32 devices in a mesh: dp: 4 (over y, x), ctx: 4 (over z), tp: 2 (over core).
Axes of the slice: x: 2, y: 2, z: 4, core: 2. Of those that a mesh axis runs over, the one named last changes fastest.
Arguments:
- xbc: bfloat16 [2048, 12288], P(('dp', 'ctx'), 'tp'), parts along dimension 0, may hold values from -6 to 6
- gate_in: bfloat16 [2048, 8192], P(('dp', 'ctx'), 'tp'), parts along dimension 0, may hold values from -6 to 6
- dt_raw: float32 [128, 2048], P('tp', ('dp', 'ctx')), parts along dimension 1, may hold values from -2 to 13.2
- dt_bias: float32 [512], P(('dp', 'tp')), parts along dimension 0, may hold values from -13 to -3
- a_log: float32 [128], P('tp'), may hold values from -0.7 to 0
- conv_weight: float32 [4, 12288], P(None, 'tp'), may hold values from -3 to 3
- conv_bias: float32 [12288], P('tp'), may hold values from -3 to 3
- skip_weight: float32 [128], P('tp'), may hold values from 0.5 to 1.5
- norm_gain: float32 [8192], P('tp'), may hold values from 0.5 to 1.5
- queries: bfloat16 [2048, 8192], P(('dp', 'ctx'), 'tp'), parts along dimension 0, may hold values from -10 to 10
- keys: bfloat16 [2048, 1024], P(('dp', 'ctx'), 'tp'), parts along dimension 0, may hold values from -6 to 6
- values: bfloat16 [2048, 1024], P(('dp', 'ctx'), 'tp'), parts along dimension 0, may hold values from -6 to 6
Outputs:
- mamba_out: bfloat16 [2048, 8192], P(('dp', 'ctx'), 'tp'), parts along dimension 0
- attn_out: bfloat16 [2048, 8192], P(('dp', 'ctx'), 'tp'), parts along dimension 0
The draws below stay inside these ranges and needn't reach their ends.
There are 4 independent parts, one for each index of `dp`. The reference program is written for one: setup_inputs(seed, part) draws one part's arguments, and reference() takes and returns one part's arrays. A program takes and returns all parts, laid end to end along the dimension named above; an argument that names none is the same for every part. Nothing has to cross between parts.
All inputs are finite; a program needn't handle non-finite values.
Results may differ from the reference program's by a relative error of at most 0.0047.
Values may be sent and summed in bfloat16 or wider, within the bound.
A program may use at most 64 MiB of HBM per device.

```python
import math
import jax
import jax.numpy as jnp
from jax import lax

MAMBA_HEAD_COUNT = 128
SSM_HEAD_DIM = 64
SSM_STATE = 256
SSM_GROUPS = 8
CONV_WIDTH = 4
SPAN_LEN = 128
QUERY_HEADS = 64
KEY_HEADS = 8
KEY_DIM = 128
SEQUENCE_LENGTH = 512
N_TP = 2


pulse_count = 6


def rate_pieces(key):
    key_bias, key_rough, key_location, key_raise, key_steady, key_steady_bias, key_target = jax.random.split(jax.random.fold_in(key, 29), 7)
    per_head_bias = jax.random.uniform(key_bias, (MAMBA_HEAD_COUNT,), jnp.float32, -13.0, -3.0)
    coarse_portion = jnp.clip(0.5 * jax.random.normal(key_rough, (MAMBA_HEAD_COUNT, SEQUENCE_LENGTH), jnp.float32), -2.0, 2.0)
    locations = jax.random.randint(key_location, (pulse_count,), 0, SEQUENCE_LENGTH)
    hit_flags = jnp.any(jnp.arange(SEQUENCE_LENGTH)[None, :] == locations[:, None], axis=0)
    pulse_raise = jax.random.uniform(key_raise, (MAMBA_HEAD_COUNT, 1), jnp.float32, -0.8, 0.2)
    steady_flags = jax.random.randint(key_steady, (MAMBA_HEAD_COUNT,), 0, 2) == 1
    steady_bias = jax.random.uniform(key_steady_bias, (MAMBA_HEAD_COUNT,), jnp.float32, -13.0, -9.0)
    steady_target = jax.random.uniform(key_target, (MAMBA_HEAD_COUNT, 1), jnp.float32, -6.6, -5.6)
    per_head_bias = jnp.where(steady_flags, steady_bias, per_head_bias)
    pulsed_rates = jnp.where(hit_flags[None, :], pulse_raise - per_head_bias[:, None], coarse_portion)
    steady_rates = steady_target - per_head_bias[:, None] + coarse_portion
    unshaped_rates = jnp.where(steady_flags[:, None], steady_rates, pulsed_rates)
    return (per_head_bias, unshaped_rates)


def draw_dt_raw(key, part):
    return rate_pieces(key)[1]


def draw_dt_bias(key, part):
    return rate_pieces(key)[0]


def drawn_pair(key):
    key_query, key_key = jax.random.split(jax.random.fold_in(key, 41), 2)
    query_shape = (SEQUENCE_LENGTH, QUERY_HEADS, KEY_DIM)
    key_shape = (SEQUENCE_LENGTH, KEY_HEADS, KEY_DIM)
    query_part = jnp.clip(2.5 * jax.random.normal(key_query, query_shape, jnp.float32), -10.0, 10.0)
    key_part = jnp.clip(jax.random.normal(key_key, key_shape, jnp.float32), -6.0, 6.0)
    return (query_part.reshape(SEQUENCE_LENGTH, -1), key_part.reshape(SEQUENCE_LENGTH, -1))


def draw_queries(key, part):
    return drawn_pair(key)[0].astype(jnp.bfloat16)


def draw_keys(key, part):
    return drawn_pair(key)[1].astype(jnp.bfloat16)


def shard_levels(rng, shape, cuts, smallest, largest):
    factor_of = 1.0
    for dim, shards_of in cuts:
        draws = jax.random.uniform(jax.random.fold_in(jax.random.fold_in(rng, 6), dim), (shards_of,), jnp.float32, smallest / len(cuts), largest / len(cuts))
        factor_of = factor_of * jnp.repeat(jnp.exp(draws), shape[dim] // shards_of).reshape((-1,) + (1,) * (len(shape) - 1 - dim))
    return factor_of


def centred(key, extent, width, bound, cuts=(), dtype=jnp.bfloat16):
    factor_of = shard_levels(key, extent, cuts, -0.22, 0.18) if cuts else 1.0
    values = jax.random.normal(key, extent, jnp.float32) * width * factor_of
    return jnp.minimum(jnp.maximum(values, -bound), bound).astype(dtype)


def setup_inputs(seed: int = 0, part: int = 0) -> dict:
    arg_keys = jax.random.split(jax.random.key(seed), 13)
    part_splits = jax.random.split(jax.random.fold_in(arg_keys[12], part), 13)
    return {
        "xbc": centred(part_splits[0], (SEQUENCE_LENGTH, MAMBA_HEAD_COUNT * SSM_HEAD_DIM + 2 * SSM_GROUPS * SSM_STATE), 1.0, 6.0, ((0, 4), (1, 2))),
        "gate_in": centred(part_splits[1], (SEQUENCE_LENGTH, MAMBA_HEAD_COUNT * SSM_HEAD_DIM), 1.0, 6.0, ((0, 4), (1, 2))),
        "dt_raw": draw_dt_raw(jax.random.fold_in(jax.random.fold_in(arg_keys[12], part), 71), part),
        "dt_bias": draw_dt_bias(jax.random.fold_in(jax.random.fold_in(arg_keys[12], part), 71), part),
        "a_log": jnp.clip(-0.7 + 0.7 * jax.random.uniform(arg_keys[4], (MAMBA_HEAD_COUNT,), jnp.float32) ** shard_levels(arg_keys[4], (MAMBA_HEAD_COUNT,), ((0, 2),), -0.2, 0.2), -0.7, 0.0),
        "conv_weight": centred(arg_keys[5], (CONV_WIDTH, MAMBA_HEAD_COUNT * SSM_HEAD_DIM + 2 * SSM_GROUPS * SSM_STATE), CONV_WIDTH ** -0.5, 3.0, ((1, 2),), jnp.float32),
        "conv_bias": centred(arg_keys[6], (MAMBA_HEAD_COUNT * SSM_HEAD_DIM + 2 * SSM_GROUPS * SSM_STATE,), 0.5, 3.0, ((0, 2),), jnp.float32),
        "skip_weight": jnp.clip(0.5 + 1.0 * jax.random.uniform(arg_keys[7], (MAMBA_HEAD_COUNT,), jnp.float32) ** shard_levels(arg_keys[7], (MAMBA_HEAD_COUNT,), ((0, 2),), -0.2, 0.2), 0.5, 1.5),
        "norm_gain": jnp.clip(1.0 + 0.1 * jax.random.normal(arg_keys[8], (MAMBA_HEAD_COUNT * SSM_HEAD_DIM,), jnp.float32), 0.5, 1.5),
        "queries": draw_queries(jax.random.fold_in(jax.random.fold_in(arg_keys[12], part), 71), part),
        "keys": draw_keys(jax.random.fold_in(jax.random.fold_in(arg_keys[12], part), 71), part),
        "values": centred(part_splits[11], (SEQUENCE_LENGTH, KEY_HEADS * KEY_DIM), 1.0, 6.0, ((0, 4), (1, 2))),
    }


eps = 1e-05
highest = lax.Precision.HIGHEST

def conv_section(xbc, conv_weight, conv_bias):
    taps_count = conv_weight.shape[0]
    row_count = xbc.shape[0]
    padded = jnp.concatenate([jnp.zeros((taps_count - 1, xbc.shape[1]), jnp.float32), xbc.astype(jnp.float32)], axis=0)
    running = jnp.zeros((row_count, xbc.shape[1]), jnp.float32) + conv_bias[None, :]
    for offset in range(taps_count):
        running = running + conv_weight[offset][None, :] * padded[offset:offset + row_count]
    return jax.nn.silu(running).astype(jnp.bfloat16)

def mamba_mixer(xbc, gate_in, dt_raw, dt_bias, a_log, conv_weight, conv_bias, skip_weight, norm_gain):
    per_group = MAMBA_HEAD_COUNT // SSM_GROUPS
    head_cols = MAMBA_HEAD_COUNT // N_TP * SSM_HEAD_DIM
    group_cols = SSM_GROUPS // N_TP * SSM_STATE
    conv_out = conv_section(xbc, conv_weight, conv_bias).reshape(SEQUENCE_LENGTH, N_TP, head_cols + 2 * group_cols)
    inputs = conv_out[:, :, :head_cols].reshape(SEQUENCE_LENGTH, MAMBA_HEAD_COUNT, SSM_HEAD_DIM)
    b_heads = jnp.repeat(conv_out[:, :, head_cols:head_cols + group_cols].reshape(SEQUENCE_LENGTH, SSM_GROUPS, SSM_STATE), per_group, axis=1)
    c_heads = jnp.repeat(conv_out[:, :, head_cols + group_cols:].reshape(SEQUENCE_LENGTH, SSM_GROUPS, SSM_STATE), per_group, axis=1)
    dt_step = jax.nn.softplus(dt_raw + dt_bias[:, None])
    log_decay = -dt_step * jnp.exp(a_log)[:, None]
    span_count = SEQUENCE_LENGTH // SPAN_LEN

    def by_span(array):
        return array.reshape((span_count, SPAN_LEN) + array.shape[1:])

    def by_span_heads(array):
        return array.reshape(MAMBA_HEAD_COUNT, span_count, SPAN_LEN).transpose(1, 0, 2)
    causal = jnp.arange(SPAN_LEN)[:, None] >= jnp.arange(SPAN_LEN)[None, :]

    def span_step(carried, pieces):
        x_span, b_span, c_span, dt_span, decay_span = pieces
        cumulative = jnp.cumsum(decay_span, axis=1)
        decay_gaps = cumulative[:, :, None] - cumulative[:, None, :]
        decay_matrix = jnp.where(causal[None], jnp.exp(jnp.where(causal[None], decay_gaps, 0.0)), 0.0)
        products = jnp.einsum('thn,shn->hts', c_span.astype(jnp.float32), b_span.astype(jnp.float32), precision=highest)
        mixing = (products * decay_matrix * dt_span[:, None, :]).astype(jnp.bfloat16)
        within_block = jnp.einsum('hts,shp->thp', mixing.astype(jnp.float32), x_span.astype(jnp.float32), precision=highest)
        tail_weight = dt_span * jnp.exp(cumulative[:, -1:] - cumulative)
        weighted = (x_span.astype(jnp.float32) * tail_weight.T[:, :, None]).astype(jnp.bfloat16)
        block_state = jnp.einsum('shn,shp->hpn', b_span.astype(jnp.float32), weighted.astype(jnp.float32), precision=highest)
        from_state = jnp.einsum('thn,hpn->thp', c_span.astype(jnp.float32), carried, precision=highest) * jnp.exp(cumulative).T[:, :, None]
        outputs = within_block + from_state + skip_weight[None, :, None] * x_span.astype(jnp.float32)
        carried = jnp.exp(cumulative[:, -1])[:, None, None] * carried + block_state
        return (carried, outputs)
    pieces = (by_span(inputs), by_span(b_heads), by_span(c_heads), by_span_heads(dt_step), by_span_heads(log_decay))
    final_state, outputs = lax.scan(span_step, jnp.zeros((MAMBA_HEAD_COUNT, SSM_HEAD_DIM, SSM_STATE), jnp.float32), pieces)
    mixer = outputs.reshape(SEQUENCE_LENGTH, MAMBA_HEAD_COUNT * SSM_HEAD_DIM) * jax.nn.silu(gate_in.astype(jnp.float32))
    grouped = mixer.reshape(SEQUENCE_LENGTH, SSM_GROUPS, -1)
    norm_scale = lax.rsqrt(lax.optimization_barrier(jnp.mean(grouped * grouped, axis=-1, keepdims=True)) + eps)
    return ((grouped * norm_scale).reshape(SEQUENCE_LENGTH, -1) * norm_gain[None, :]).astype(jnp.bfloat16)

def attention(queries, keys, values):
    repeat_count = QUERY_HEADS // KEY_HEADS
    score_scale = 1.0 / math.sqrt(KEY_DIM)
    query_heads = queries.reshape(SEQUENCE_LENGTH, QUERY_HEADS, KEY_DIM).transpose(1, 0, 2)
    key_heads = jnp.repeat(keys.reshape(SEQUENCE_LENGTH, KEY_HEADS, KEY_DIM).transpose(1, 0, 2), repeat_count, axis=0)
    value_heads = jnp.repeat(values.reshape(SEQUENCE_LENGTH, KEY_HEADS, KEY_DIM).transpose(1, 0, 2), repeat_count, axis=0)
    causal = jnp.arange(SEQUENCE_LENGTH)[:, None] >= jnp.arange(SEQUENCE_LENGTH)[None, :]

    def one_head(pieces):
        query_rows, key_rows, value_rows = pieces
        scores = jnp.dot(query_rows, key_rows.T, preferred_element_type=jnp.float32) * score_scale
        row_top = lax.optimization_barrier(jnp.max(jnp.where(causal, scores, -1e+30), axis=1, keepdims=True))
        weights = jnp.where(causal, jnp.exp(scores - row_top), 0.0)
        row_total = lax.optimization_barrier(jnp.sum(weights, axis=1, keepdims=True))
        return jnp.dot(weights.astype(jnp.bfloat16), value_rows, preferred_element_type=jnp.float32) / row_total
    heads_out = lax.map(one_head, (query_heads, key_heads, value_heads))
    return heads_out.transpose(1, 0, 2).reshape(SEQUENCE_LENGTH, -1).astype(jnp.bfloat16)

def reference(xbc, gate_in, dt_raw, dt_bias, a_log, conv_weight, conv_bias, skip_weight, norm_gain, queries, keys, values):
    mamba_out = mamba_mixer(xbc, gate_in, dt_raw, dt_bias, a_log, conv_weight, conv_bias, skip_weight, norm_gain)
    attn_out = attention(queries, keys, values)
    return (mamba_out, attn_out)
```

```python
import functools
import math

import jax
import jax.numpy as jnp
from jax import lax
from jax.experimental import pallas as pl
from jax.experimental.pallas import tpu as pltpu
from jax.sharding import PartitionSpec as P

P_DIM = 64
N_STATE = 256
KEY_DIM = 128
CHUNK = 256
RIM = 16
EPS = 1e-05
NEG = -1e30
F32 = jnp.float32
BF16 = jnp.bfloat16


def dot(a, b):
    return jnp.dot(a, b, preferred_element_type=F32)


def dot_nt(a, b):
    return lax.dot_general(a, b, (((1,), (1,)), ((), ())), preferred_element_type=F32)


def silu(v):
    return v / (1.0 + jnp.exp(-v))


def log1p_unit(e):
    z = e / (2.0 + e)
    z2 = z * z
    acc = jnp.full_like(z, 1.0 / 17.0)
    for k in (15, 13, 11, 9, 7, 5, 3, 1):
        acc = acc * z2 + 1.0 / k
    return 2.0 * z * acc


def kernel(
    n,
    xbc,
    gate,
    dt_raw,
    dt_bias,
    a_log,
    conv_w,
    conv_b,
    skip,
    gain,
    queries,
    keys,
    values,
    mamba_out,
    attn_out,
    rim,
    xc,
    kbuf,
    vbuf,
    dt_row,
    cum_row,
    ecum_x,
    spread,
    s_own,
    h_in,
    h_out,
    y_acc,
    rim_send,
    rim_recv,
    k_send,
    k_recv,
    v_send,
    v_recv,
    h_send,
    h_recv,
):
    me = lax.axis_index("ctx")
    rows = xbc.shape[0]
    heads = dt_raw.shape[0]
    head_cols = heads * P_DIM
    groups = (xbc.shape[1] - head_cols) // (2 * N_STATE)
    per_group = heads // groups
    gcols = per_group * P_DIM
    per_chunks = gcols // CHUNK
    chunks = groups * per_chunks
    taps = conv_w.shape[0]
    kv_heads = keys.shape[1] // KEY_DIM
    repeat = queries.shape[1] // keys.shape[1]
    has_next = me < n - 1
    has_prev = me > 0
    right = me + 1

    def remote(src, dst, send, recv):
        return pltpu.make_async_remote_copy(
            src_ref=src,
            dst_ref=dst,
            send_sem=send,
            recv_sem=recv,
            device_id={"ctx": right},
            device_id_type=pl.DeviceIdType.MESH,
        )

    barrier = pltpu.get_barrier_semaphore()

    @pl.when(has_prev)
    def _():
        pl.semaphore_signal(
            barrier, inc=1, device_id={"ctx": me - 1}, device_id_type=pl.DeviceIdType.MESH
        )

    @pl.when(has_next)
    def _():
        pl.semaphore_wait(barrier, 1)

    def rim_copy():
        return remote(xbc.at[pl.ds(rows - RIM, RIM), :], rim, rim_send, rim_recv)

    def own_kv():
        return (
            remote(keys, kbuf.at[me], k_send.at[me], k_recv.at[me]),
            remote(values, vbuf.at[me], v_send.at[me], v_recv.at[me]),
        )

    def kv_copy(block):
        return (
            remote(kbuf.at[block], kbuf.at[block], k_send.at[block], k_recv.at[block]),
            remote(vbuf.at[block], vbuf.at[block], v_send.at[block], v_recv.at[block]),
        )

    def h_copy(c):
        return remote(h_out.at[c], h_in.at[c], h_send.at[c], h_recv.at[c])

    @pl.when(has_next)
    def _():
        rim_copy().start()
        for copy in own_kv():
            copy.start()

    kbuf[me] = keys[...]
    vbuf[me] = values[...]

    def clear(j, carry):
        @pl.when(j > me)
        def _():
            kbuf[j] = jnp.zeros(keys.shape, BF16)
            vbuf[j] = jnp.zeros(values.shape, BF16)

        return carry

    lax.fori_loop(0, n, clear, 0)

    def column(ref):
        return jnp.transpose(jnp.broadcast_to(ref[...], (rows, heads)))

    pre = dt_raw[...] + column(dt_bias)
    dt = jnp.maximum(pre, 0.0) + log1p_unit(jnp.exp(-jnp.abs(pre)))
    cum = -dt * jnp.exp(column(a_log))
    lane = lax.broadcasted_iota(jnp.int32, (heads, rows), 1)
    step = 1
    while step < rows:
        cum = cum + jnp.where(lane >= step, pltpu.roll(cum, step, 1), 0.0)
        step *= 2
    dt_row[...] = dt
    cum_row[...] = cum
    spread_row = lax.broadcasted_iota(jnp.int32, (3 * per_group, gcols), 0)
    spread_col = lax.broadcasted_iota(jnp.int32, (3 * per_group, gcols), 1)
    hit = lax.rem(spread_row, per_group) == spread_col // P_DIM
    spread[...] = jnp.where(hit, 1.0, 0.0).astype(BF16)

    def expand(v):
        hi = v.astype(BF16).astype(F32)
        rest = v - hi
        mid = rest.astype(BF16).astype(F32)
        low = rest - mid
        parts = jnp.transpose(jnp.concatenate([hi, mid, low], axis=0))
        return dot(parts.astype(BF16), spread[...])

    @pl.when(has_prev)
    def _():
        rim_copy().wait_recv()

    @pl.when(me == 0)
    def _():
        rim[...] = jnp.zeros(rim.shape, BF16)

    def conv_tile(start, width):
        cols = pl.ds(pl.multiple_of(start, 256), width)
        ext = jnp.concatenate([rim[:, cols].astype(F32), xbc[:, cols].astype(F32)], axis=0)
        acc = jnp.broadcast_to(conv_b[:, cols], (rows, width))
        for tap in range(taps):
            by = taps - 1 - tap
            moved = ext if by == 0 else pltpu.roll(ext, by, 0)
            acc = acc + conv_w[tap : tap + 1, cols] * moved[RIM:]
        out = silu(acc)
        xc[:, cols] = out.astype(BF16)
        return out

    def group_rows(g):
        return pl.ds(pl.multiple_of(g * per_group, per_group), per_group)

    def first(g, carry):
        b_part = conv_tile(head_cols + g * N_STATE, N_STATE)
        b_turned = jnp.transpose(b_part).astype(BF16)
        cum_g = cum_row[group_rows(g), :]
        dt_g = dt_row[group_rows(g), :]
        last = jnp.broadcast_to(cum_g[:, rows - 1 :], cum_g.shape)
        tail = expand(dt_g * jnp.exp(last - cum_g))
        for i in range(per_chunks):
            c = g * per_chunks + i
            x_part = conv_tile(c * CHUNK, CHUNK).astype(BF16).astype(F32)
            weighted = (x_part * tail[:, i * CHUNK : (i + 1) * CHUNK]).astype(BF16)
            own = dot(b_turned, weighted)
            s_own[c] = own

            @pl.when(me == 0)
            def _():
                h_out[c] = own.astype(BF16)
                h_copy(c).start()

        ecum_x[:, pl.ds(pl.multiple_of(g * gcols, gcols), gcols)] = expand(jnp.exp(cum_g))
        conv_tile(head_cols + (groups + g) * N_STATE, N_STATE)
        return carry

    lax.fori_loop(0, groups, first, 0)

    def within(g):
        b_part = xc[:, pl.ds(pl.multiple_of(head_cols + g * N_STATE, N_STATE), N_STATE)]
        c_part = xc[:, pl.ds(pl.multiple_of(head_cols + (groups + g) * N_STATE, N_STATE), N_STATE)]
        products = dot_nt(c_part, b_part)
        cum_g = cum_row[group_rows(g), :]
        dt_g = dt_row[group_rows(g), :]
        cum_t = jnp.transpose(cum_g)
        t_pos = lax.broadcasted_iota(jnp.int32, (rows, rows), 0)
        s_pos = lax.broadcasted_iota(jnp.int32, (rows, rows), 1)
        causal = s_pos <= t_pos
        low_half = lax.broadcasted_iota(jnp.int32, (rows, 2 * P_DIM), 1) < P_DIM
        for pair in range(per_group // 2):
            mixes = []
            for j in (2 * pair, 2 * pair + 1):
                gap = cum_t[:, j : j + 1] - cum_g[j : j + 1, :]
                decay = jnp.exp(jnp.where(causal, gap, NEG))
                mixes.append((products * decay * dt_g[j : j + 1, :]).astype(BF16))
            cols = pl.ds(pl.multiple_of(g * gcols + pair * 2 * P_DIM, 2 * P_DIM), 2 * P_DIM)
            x_pair = xc[:, cols].astype(F32)
            x_two = jnp.concatenate(
                [jnp.where(low_half, x_pair, 0.0), jnp.where(low_half, 0.0, x_pair)], axis=0
            ).astype(BF16)
            scale = jnp.where(
                low_half, skip[g * per_group + 2 * pair], skip[g * per_group + 2 * pair + 1]
            )
            y_acc[:, cols] = dot(jnp.concatenate(mixes, axis=1), x_two) + scale * x_pair

    pieces = kv_heads * 2
    piece_heads = repeat // 2
    log2_scale = 1.4426950408889634 / math.sqrt(KEY_DIM)

    def attend(piece):
        kv_cols = pl.ds(pl.multiple_of((piece // 2) * KEY_DIM, KEY_DIM), KEY_DIM)
        k_all = jnp.concatenate([kbuf[j, :, kv_cols] for j in range(n)], axis=0)
        v_all = jnp.concatenate([vbuf[j, :, kv_cols] for j in range(n)], axis=0)
        q_pos = me * rows + lax.broadcasted_iota(jnp.int32, (rows, n * rows), 0)
        k_pos = lax.broadcasted_iota(jnp.int32, (rows, n * rows), 1)
        allowed = k_pos <= q_pos
        for j in range(piece_heads):
            start = (piece * piece_heads + j) * KEY_DIM
            cols = pl.ds(pl.multiple_of(start, KEY_DIM), KEY_DIM)
            scores = jnp.where(allowed, dot_nt(queries[:, cols], k_all), NEG)
            top = jnp.max(scores, axis=1, keepdims=True)
            probs = jnp.exp2((scores - top) * log2_scale)
            total = jnp.sum(probs, axis=1, keepdims=True)
            attn_out[:, cols] = (dot(probs.astype(BF16), v_all) / total).astype(BF16)

    def relay(s):
        block = me - 1 - s

        @pl.when(block >= 0)
        def _():
            for copy in kv_copy(block):
                copy.wait_recv()

            @pl.when(has_next)
            def _():
                for copy in kv_copy(block):
                    copy.start()

    def finish(g):
        cols = pl.ds(pl.multiple_of(g * gcols, gcols), gcols)
        v = y_acc[:, cols] * silu(gate[:, cols].astype(F32))
        scale = lax.rsqrt(jnp.mean(v * v, axis=1, keepdims=True) + EPS)
        mamba_out[:, cols] = (v * scale * gain[:, cols]).astype(BF16)

    def chain(c, carry):
        g = c // per_chunks
        cols = pl.ds(pl.multiple_of(c * CHUNK, CHUNK), CHUNK)

        @pl.when(c < n - 1)
        def _():
            relay(c)

        @pl.when(has_prev)
        def _():
            h_copy(c).wait_recv()

            @pl.when(has_next)
            def _():
                total = ecum_x[rows - 1 : rows, cols]
                h_out[c] = (total * h_in[c].astype(F32) + s_own[c]).astype(BF16)
                h_copy(c).start()

        @pl.when(c < groups)
        def _():
            within(c)

        @pl.when(has_prev)
        def _():
            c_cols = pl.ds(
                pl.multiple_of(head_cols + (groups + g) * N_STATE, N_STATE), N_STATE
            )
            y_acc[:, cols] += ecum_x[:, cols] * dot(xc[:, c_cols], h_in[c])

        @pl.when(lax.rem(c, per_chunks) == per_chunks - 1)
        def _():
            finish(g)

        piece = c - lead

        @pl.when((piece >= 0) & (piece < pieces))
        def _():
            attend(piece)

        return carry

    lead = max(n - 1, groups)
    lax.fori_loop(0, chunks, chain, 0)
    for s in range(chunks, n - 1):
        relay(s)

    def rest(piece, carry):
        attend(piece)
        return carry

    if chunks - lead < pieces:
        lax.fori_loop(max(chunks - lead, 0), pieces, rest, 0)

    @pl.when(has_next)
    def _():
        rim_copy().wait_send()
        for copy in own_kv():
            copy.wait_send()

        def sent(c, carry):
            h_copy(c).wait_send()
            return carry

        lax.fori_loop(0, chunks, sent, 0)

        def sent_kv(block, carry):
            @pl.when(block < me)
            def _():
                for copy in kv_copy(block):
                    copy.wait_send()

            return carry

        lax.fori_loop(0, n, sent_kv, 0)


def shards(
    n,
    xbc,
    gate_in,
    dt_raw,
    dt_bias,
    a_log,
    conv_weight,
    conv_bias,
    skip_weight,
    norm_gain,
    queries,
    keys,
    values,
):
    rows = xbc.shape[0]
    heads = dt_raw.shape[0]
    head_cols = heads * P_DIM
    groups = (xbc.shape[1] - head_cols) // (2 * N_STATE)
    per_group = heads // groups
    chunks = head_cols // CHUNK
    vmem = pl.BlockSpec(memory_space=pltpu.VMEM)
    smem = pl.BlockSpec(memory_space=pltpu.SMEM)
    dma = pltpu.SemaphoreType.DMA
    return pl.pallas_call(
        functools.partial(kernel, n),
        out_shape=(
            jax.ShapeDtypeStruct((rows, head_cols), BF16),
            jax.ShapeDtypeStruct(queries.shape, BF16),
        ),
        in_specs=[vmem] * 7 + [smem] + [vmem] * 4,
        out_specs=(vmem, vmem),
        scratch_shapes=[
            pltpu.VMEM((RIM, xbc.shape[1]), BF16),
            pltpu.VMEM(xbc.shape, BF16),
            pltpu.VMEM((n,) + keys.shape, BF16),
            pltpu.VMEM((n,) + values.shape, BF16),
            pltpu.VMEM(dt_raw.shape, F32),
            pltpu.VMEM(dt_raw.shape, F32),
            pltpu.VMEM((rows, head_cols), F32),
            pltpu.VMEM((3 * per_group, per_group * P_DIM), BF16),
            pltpu.VMEM((chunks, N_STATE, CHUNK), F32),
            pltpu.VMEM((chunks, N_STATE, CHUNK), BF16),
            pltpu.VMEM((chunks, N_STATE, CHUNK), BF16),
            pltpu.VMEM((rows, head_cols), F32),
            dma,
            dma,
            dma((n,)),
            dma((n,)),
            dma((n,)),
            dma((n,)),
            dma((chunks,)),
            dma((chunks,)),
        ],
        compiler_params=pltpu.CompilerParams(
            collective_id=0, has_side_effects=True, vmem_limit_bytes=48 * 1024 * 1024
        ),
        name="mixers",
    )(
        xbc,
        gate_in,
        dt_raw,
        dt_bias.reshape(1, -1),
        a_log.reshape(1, -1),
        conv_weight,
        conv_bias.reshape(1, -1),
        skip_weight,
        norm_gain.reshape(1, -1),
        queries,
        keys,
        values,
    )


def solution(mesh):
    placed = (
        P(("dp", "ctx"), "tp"),
        P(("dp", "ctx"), "tp"),
        P("tp", ("dp", "ctx")),
        P(("dp", "tp")),
        P("tp"),
        P(None, "tp"),
        P("tp"),
        P("tp"),
        P("tp"),
        P(("dp", "ctx"), "tp"),
        P(("dp", "ctx"), "tp"),
        P(("dp", "ctx"), "tp"),
    )
    return jax.shard_map(
        functools.partial(shards, mesh.shape["ctx"]),
        mesh=mesh,
        in_specs=placed,
        out_specs=(P(("dp", "ctx"), "tp"), P(("dp", "ctx"), "tp")),
        check_vma=False,
    )
```

```python
import functools
import math

import jax
import jax.numpy as jnp
from jax import lax
from jax.experimental import pallas as pl
from jax.experimental.pallas import tpu as pltpu
from jax.sharding import PartitionSpec as P

P_DIM = 64
N_STATE = 256
KEY_DIM = 128
CHUNK = 256
RIM = 16
RIM_WIDTH = 384
EPS = 1e-05
NEG = -1e30
F32 = jnp.float32
BF16 = jnp.bfloat16


def dot(a, b):
    return jnp.dot(a, b, preferred_element_type=F32)


def dot_nt(a, b):
    return lax.dot_general(a, b, (((1,), (1,)), ((), ())), preferred_element_type=F32)


def silu(v):
    return v / (1.0 + jnp.exp(-v))


def log1p_unit(e):
    z = e / (2.0 + e)
    z2 = z * z
    acc = jnp.full_like(z, 1.0 / 17.0)
    for k in (15, 13, 11, 9, 7, 5, 3, 1):
        acc = acc * z2 + 1.0 / k
    return 2.0 * z * acc


def kernel(
    n,
    xbc_hbm,
    gate_hbm,
    dt_hbm,
    bias_hbm,
    alog_hbm,
    convw_hbm,
    convb_hbm,
    skip_hbm,
    gain_hbm,
    queries_hbm,
    keys_hbm,
    values_hbm,
    mamba_out,
    attn_out,
    xbc,
    gate,
    dt_raw,
    dt_bias,
    a_log,
    conv_w,
    conv_b,
    skip,
    gain,
    queries,
    keys,
    values,
    rim_wide,
    rim_tall,
    rim_src,
    rim_dst,
    xc,
    kbuf,
    vbuf,
    dt_row,
    cum_row,
    skip_row,
    ecum_x,
    spread,
    s_own,
    h_in,
    h_out,
    r_in,
    r_out,
    c_next,
    y_acc,
    in_sems,
    rim_send,
    rim_recv,
    k_send,
    k_recv,
    v_send,
    v_recv,
    h_send,
    h_recv,
    r_send,
    r_recv,
    c_send,
    c_recv,
):
    me = lax.axis_index("ctx")
    rows = xbc.shape[0]
    heads = dt_raw.shape[0]
    head_cols = heads * P_DIM
    groups = (xbc.shape[1] - head_cols) // (2 * N_STATE)
    per_group = heads // groups
    gcols = per_group * P_DIM
    per_chunks = gcols // CHUNK
    chunks = groups * per_chunks
    taps = conv_w.shape[0]
    kv_heads = keys.shape[1] // KEY_DIM
    repeat = queries.shape[1] // keys.shape[1]
    has_next = me < n - 1
    has_prev = me > 0
    right = me + 1
    is_last = me == n - 1
    before_last = me == n - 2
    pieces_wide = xbc.shape[1] // RIM_WIDTH

    pairs = (
        (xbc_hbm, xbc),
        (dt_hbm, dt_raw),
        (bias_hbm, dt_bias),
        (alog_hbm, a_log),
        (convw_hbm, conv_w),
        (convb_hbm, conv_b),
        (skip_hbm, skip),
        (keys_hbm, keys),
        (values_hbm, values),
        (queries_hbm, queries),
        (gate_hbm, gate),
        (gain_hbm, gain),
    )
    loads = [pltpu.make_async_copy(a, b, in_sems.at[i]) for i, (a, b) in enumerate(pairs)]
    for load in loads:
        load.start()

    def remote(src, dst, send, recv, to):
        return pltpu.make_async_remote_copy(
            src_ref=src,
            dst_ref=dst,
            send_sem=send,
            recv_sem=recv,
            device_id={"ctx": to},
            device_id_type=pl.DeviceIdType.MESH,
        )

    barrier = pltpu.get_barrier_semaphore()

    @pl.when(has_prev)
    def _():
        pl.semaphore_signal(
            barrier, inc=1, device_id={"ctx": me - 1}, device_id_type=pl.DeviceIdType.MESH
        )

    @pl.when(before_last)
    def _():
        pl.semaphore_signal(
            barrier, inc=1, device_id={"ctx": me + 1}, device_id_type=pl.DeviceIdType.MESH
        )

    def rim_copy():
        return remote(rim_src, rim_dst, rim_send, rim_recv, right)

    def own_kv():
        return (
            remote(keys_hbm, kbuf.at[me], k_send.at[me], k_recv.at[me], right),
            remote(values_hbm, vbuf.at[me], v_send.at[me], v_recv.at[me], right),
        )

    def kv_copy(block):
        return (
            remote(kbuf.at[block], kbuf.at[block], k_send.at[block], k_recv.at[block], right),
            remote(vbuf.at[block], vbuf.at[block], v_send.at[block], v_recv.at[block], right),
        )

    def h_copy(c):
        return remote(h_out.at[c], h_in.at[c], h_send.at[c], h_recv.at[c], right)

    def r_copy(c):
        return remote(r_out.at[c], r_in.at[c], r_send.at[c], r_recv.at[c], right)

    def c_copy():
        return remote(
            xc.at[:, pl.ds(head_cols + groups * N_STATE, groups * N_STATE)],
            c_next,
            c_send,
            c_recv,
            me - 1,
        )

    @pl.when(has_next | is_last)
    def _():
        pl.semaphore_wait(barrier, 1)

    loads[0].wait()

    @pl.when(has_next)
    def _():
        last = xbc[rows - RIM :, :].astype(F32)
        for p in range(pieces_wide):
            rim_tall[p * 3 : p * 3 + 3, :] = last[
                RIM - 3 :, p * RIM_WIDTH : (p + 1) * RIM_WIDTH
            ]
        rim_src[...] = rim_tall[...].astype(BF16)
        rim_copy().start()
        for copy in own_kv():
            copy.start()

    def clear(j, carry):
        @pl.when(j > me)
        def _():
            kbuf[j] = jnp.zeros(keys.shape, BF16)
            vbuf[j] = jnp.zeros(values.shape, BF16)

        return carry

    lax.fori_loop(0, n, clear, 0)
    for load in loads[1:7]:
        load.wait()

    def column(ref):
        return jnp.transpose(jnp.broadcast_to(ref[...], (rows, heads)))

    pre = dt_raw[...] + column(dt_bias)
    dt = jnp.maximum(pre, 0.0) + log1p_unit(jnp.exp(-jnp.abs(pre)))
    cum = -dt * jnp.exp(column(a_log))
    lane = lax.broadcasted_iota(jnp.int32, (heads, rows), 1)
    step = 1
    while step < rows:
        cum = cum + jnp.where(lane >= step, pltpu.roll(cum, step, 1), 0.0)
        step *= 2
    skip_row[...] = column(skip)
    dt_row[...] = dt
    cum_row[...] = cum
    spread_row = lax.broadcasted_iota(jnp.int32, (3 * per_group, gcols), 0)
    spread_col = lax.broadcasted_iota(jnp.int32, (3 * per_group, gcols), 1)
    hit = lax.rem(spread_row, per_group) == spread_col // P_DIM
    spread[...] = jnp.where(hit, 1.0, 0.0).astype(BF16)

    def expand(v):
        hi = v.astype(BF16).astype(F32)
        rest = v - hi
        mid = rest.astype(BF16).astype(F32)
        low = rest - mid
        parts = jnp.transpose(jnp.concatenate([hi, mid, low], axis=0))
        return dot(parts.astype(BF16), spread[...])

    rim_wide[...] = jnp.zeros(rim_wide.shape, F32)

    @pl.when(has_prev)
    def _():
        rim_copy().wait_recv()
        rim_tall[...] = rim_dst[...].astype(F32)
        for p in range(pieces_wide):
            rim_wide[5:, p * RIM_WIDTH : (p + 1) * RIM_WIDTH] = rim_tall[p * 3 : p * 3 + 3, :]

    def conv_tile(start, width):
        cols = pl.ds(pl.multiple_of(start, 256), width)
        ext = jnp.concatenate([rim_wide[:, cols], xbc[:, cols].astype(F32)], axis=0)
        acc = jnp.broadcast_to(conv_b[:, cols], (rows, width))
        for tap in range(taps):
            by = taps - 1 - tap
            moved = ext if by == 0 else pltpu.roll(ext, by, 0)
            acc = acc + conv_w[tap : tap + 1, cols] * moved[8:]
        out = silu(acc)
        xc[:, cols] = out.astype(BF16)
        return out

    def relay(s):
        block = me - 1 - s

        @pl.when(block >= 0)
        def _():
            for copy in kv_copy(block):
                copy.wait_recv()

            @pl.when(has_next)
            def _():
                for copy in kv_copy(block):
                    copy.start()

    def group_rows(g):
        return pl.ds(pl.multiple_of(g * per_group, per_group), per_group)

    def first(g, carry):
        b_part = conv_tile(head_cols + g * N_STATE, N_STATE)
        b_turned = jnp.transpose(b_part).astype(BF16)
        cum_g = cum_row[group_rows(g), :]
        dt_g = dt_row[group_rows(g), :]
        last = jnp.broadcast_to(cum_g[:, rows - 1 :], cum_g.shape)
        tail = expand(dt_g * jnp.exp(last - cum_g))
        for i in range(per_chunks):
            c = g * per_chunks + i
            x_part = conv_tile(c * CHUNK, CHUNK).astype(BF16).astype(F32)
            weighted = (x_part * tail[:, i * CHUNK : (i + 1) * CHUNK]).astype(BF16)
            own = dot(b_turned, weighted)
            s_own[c] = own

            @pl.when(me == 0)
            def _():
                h_out[c] = own.astype(BF16)
                h_copy(c).start()

        ecum_x[:, pl.ds(pl.multiple_of(g * gcols, gcols), gcols)] = expand(jnp.exp(cum_g))
        conv_tile(head_cols + (groups + g) * N_STATE, N_STATE)

        @pl.when(g == max(groups - 2, 0))
        def _():
            relay(0)

        return carry

    lax.fori_loop(0, groups, first, 0)

    @pl.when(is_last)
    def _():
        c_copy().start()

    for load in loads[7:]:
        load.wait()
    kbuf[me] = keys[...]
    vbuf[me] = values[...]

    def within(g):
        b_part = xc[:, pl.ds(pl.multiple_of(head_cols + g * N_STATE, N_STATE), N_STATE)]
        c_part = xc[:, pl.ds(pl.multiple_of(head_cols + (groups + g) * N_STATE, N_STATE), N_STATE)]
        products = dot_nt(c_part, b_part)
        cum_g = cum_row[group_rows(g), :]
        dt_g = dt_row[group_rows(g), :]
        skip_g = skip_row[group_rows(g), :]
        cum_t = jnp.transpose(cum_g)
        t_pos = lax.broadcasted_iota(jnp.int32, (rows, rows), 0)
        s_pos = lax.broadcasted_iota(jnp.int32, (rows, rows), 1)
        causal = s_pos <= t_pos
        low_half = lax.broadcasted_iota(jnp.int32, (rows, 2 * P_DIM), 1) < P_DIM
        for pair in range(per_group // 2):
            mixes = []
            for j in (2 * pair, 2 * pair + 1):
                gap = cum_t[:, j : j + 1] - cum_g[j : j + 1, :]
                decay = jnp.exp(jnp.where(causal, gap, NEG))
                mixes.append((products * decay * dt_g[j : j + 1, :]).astype(BF16))
            cols = pl.ds(pl.multiple_of(g * gcols + pair * 2 * P_DIM, 2 * P_DIM), 2 * P_DIM)
            x_pair = xc[:, cols].astype(F32)
            x_two = jnp.concatenate(
                [jnp.where(low_half, x_pair, 0.0), jnp.where(low_half, 0.0, x_pair)], axis=0
            ).astype(BF16)
            scale = jnp.where(
                low_half[:1], skip_g[2 * pair : 2 * pair + 1], skip_g[2 * pair + 1 : 2 * pair + 2]
            )
            y_acc[:, cols] = dot(jnp.concatenate(mixes, axis=1), x_two) + scale * x_pair

    pieces = kv_heads * 2
    piece_heads = repeat // 2
    log2_scale = 1.4426950408889634 / math.sqrt(KEY_DIM)

    def attend(piece):
        kv_cols = pl.ds(pl.multiple_of((piece // 2) * KEY_DIM, KEY_DIM), KEY_DIM)
        k_all = jnp.concatenate([kbuf[j, :, kv_cols] for j in range(n)], axis=0)
        v_all = jnp.concatenate([vbuf[j, :, kv_cols] for j in range(n)], axis=0)
        q_pos = me * rows + lax.broadcasted_iota(jnp.int32, (rows, n * rows), 0)
        k_pos = lax.broadcasted_iota(jnp.int32, (rows, n * rows), 1)
        allowed = k_pos <= q_pos
        for j in range(piece_heads):
            start = (piece * piece_heads + j) * KEY_DIM
            cols = pl.ds(pl.multiple_of(start, KEY_DIM), KEY_DIM)
            scores = jnp.where(allowed, dot_nt(queries[:, cols], k_all), NEG)
            top = jnp.max(scores, axis=1, keepdims=True)
            probs = jnp.exp2((scores - top) * log2_scale)
            total = jnp.sum(probs, axis=1, keepdims=True)
            attn_out[:, cols] = (dot(probs.astype(BF16), v_all) / total).astype(BF16)

    def finish(g):
        cols = pl.ds(pl.multiple_of(g * gcols, gcols), gcols)
        v = y_acc[:, cols] * silu(gate[:, cols].astype(F32))
        scale = lax.rsqrt(jnp.mean(v * v, axis=1, keepdims=True) + EPS)
        mamba_out[:, cols] = (v * scale * gain[:, cols]).astype(BF16)

    def chain(c, carry):
        g = c // per_chunks
        cols = pl.ds(pl.multiple_of(c * CHUNK, CHUNK), CHUNK)
        c_cols = pl.ds(pl.multiple_of(head_cols + (groups + g) * N_STATE, N_STATE), N_STATE)
        n_cols = pl.ds(pl.multiple_of(g * N_STATE, N_STATE), N_STATE)

        @pl.when((c >= 1) & (c < n - 1))
        def _():
            relay(c)

        def passed():
            total = ecum_x[rows - 1 : rows, cols]
            return (total * h_in[c].astype(F32) + s_own[c]).astype(BF16)

        @pl.when(has_prev & has_next)
        def _():
            h_copy(c).wait_recv()

        @pl.when(has_prev & (me < n - 2))
        def _():
            h_out[c] = passed()
            h_copy(c).start()

        @pl.when(before_last)
        def _():
            @pl.when(c == 0)
            def _():
                c_copy().wait_recv()

            r_out[c] = dot(c_next[:, n_cols], passed()).astype(BF16)
            r_copy(c).start()

        @pl.when(c < groups)
        def _():
            within(c)

        @pl.when(has_prev & has_next)
        def _():
            y_acc[:, cols] += ecum_x[:, cols] * dot(xc[:, c_cols], h_in[c])

        @pl.when(is_last)
        def _():
            r_copy(c).wait_recv()
            y_acc[:, cols] += ecum_x[:, cols] * r_in[c].astype(F32)

        @pl.when(lax.rem(c, per_chunks) == per_chunks - 1)
        def _():
            finish(g)

        piece = c - lead

        @pl.when((piece >= 0) & (piece < pieces))
        def _():
            attend(piece)

        return carry

    lead = max(n - 1, groups)
    lax.fori_loop(0, chunks, chain, 0)
    for s in range(max(chunks, 1), n - 1):
        relay(s)

    def rest(piece, carry):
        attend(piece)
        return carry

    if chunks - lead < pieces:
        lax.fori_loop(max(chunks - lead, 0), pieces, rest, 0)

    @pl.when(has_next)
    def _():
        rim_copy().wait_send()
        for copy in own_kv():
            copy.wait_send()

        def sent_kv(block, carry):
            @pl.when(block < me)
            def _():
                for copy in kv_copy(block):
                    copy.wait_send()

            return carry

        lax.fori_loop(0, n, sent_kv, 0)

    def sent_h(c, carry):
        h_copy(c).wait_send()
        return carry

    def sent_r(c, carry):
        r_copy(c).wait_send()
        return carry

    @pl.when(me < n - 2)
    def _():
        lax.fori_loop(0, chunks, sent_h, 0)

    @pl.when(before_last)
    def _():
        lax.fori_loop(0, chunks, sent_r, 0)

    @pl.when(is_last)
    def _():
        c_copy().wait_send()


def shards(
    n,
    xbc,
    gate_in,
    dt_raw,
    dt_bias,
    a_log,
    conv_weight,
    conv_bias,
    skip_weight,
    norm_gain,
    queries,
    keys,
    values,
):
    rows = xbc.shape[0]
    heads = dt_raw.shape[0]
    head_cols = heads * P_DIM
    groups = (xbc.shape[1] - head_cols) // (2 * N_STATE)
    per_group = heads // groups
    chunks = head_cols // CHUNK
    vmem = pl.BlockSpec(memory_space=pltpu.VMEM)
    hbm = pl.BlockSpec(memory_space=pltpu.HBM)
    dma = pltpu.SemaphoreType.DMA
    args = (
        xbc,
        gate_in,
        dt_raw,
        dt_bias.reshape(1, -1),
        a_log.reshape(1, -1),
        conv_weight,
        conv_bias.reshape(1, -1),
        skip_weight.reshape(1, -1),
        norm_gain.reshape(1, -1),
        queries,
        keys,
        values,
    )
    rim_rows = -(-(3 * (xbc.shape[1] // RIM_WIDTH)) // RIM) * RIM
    return pl.pallas_call(
        functools.partial(kernel, n),
        out_shape=(
            jax.ShapeDtypeStruct((rows, head_cols), BF16),
            jax.ShapeDtypeStruct(queries.shape, BF16),
        ),
        in_specs=[hbm] * len(args),
        out_specs=(vmem, vmem),
        scratch_shapes=[pltpu.VMEM(a.shape, a.dtype) for a in args]
        + [
            pltpu.VMEM((8, xbc.shape[1]), F32),
            pltpu.VMEM((rim_rows, RIM_WIDTH), F32),
            pltpu.VMEM((rim_rows, RIM_WIDTH), BF16),
            pltpu.VMEM((rim_rows, RIM_WIDTH), BF16),
            pltpu.VMEM(xbc.shape, BF16),
            pltpu.VMEM((n,) + keys.shape, BF16),
            pltpu.VMEM((n,) + values.shape, BF16),
            pltpu.VMEM(dt_raw.shape, F32),
            pltpu.VMEM(dt_raw.shape, F32),
            pltpu.VMEM(dt_raw.shape, F32),
            pltpu.VMEM((rows, head_cols), F32),
            pltpu.VMEM((3 * per_group, per_group * P_DIM), BF16),
            pltpu.VMEM((chunks, N_STATE, CHUNK), F32),
            pltpu.VMEM((chunks, N_STATE, CHUNK), BF16),
            pltpu.VMEM((chunks, N_STATE, CHUNK), BF16),
            pltpu.VMEM((chunks, rows, CHUNK), BF16),
            pltpu.VMEM((chunks, rows, CHUNK), BF16),
            pltpu.VMEM((rows, groups * N_STATE), BF16),
            pltpu.VMEM((rows, head_cols), F32),
            dma((len(args),)),
            dma,
            dma,
            dma((n,)),
            dma((n,)),
            dma((n,)),
            dma((n,)),
            dma((chunks,)),
            dma((chunks,)),
            dma((chunks,)),
            dma((chunks,)),
            dma,
            dma,
        ],
        compiler_params=pltpu.CompilerParams(
            collective_id=0, has_side_effects=True, vmem_limit_bytes=48 * 1024 * 1024
        ),
        name="mixers",
    )(*args)


def solution(mesh):
    placed = (
        P(("dp", "ctx"), "tp"),
        P(("dp", "ctx"), "tp"),
        P("tp", ("dp", "ctx")),
        P(("dp", "tp")),
        P("tp"),
        P(None, "tp"),
        P("tp"),
        P("tp"),
        P("tp"),
        P(("dp", "ctx"), "tp"),
        P(("dp", "ctx"), "tp"),
        P(("dp", "ctx"), "tp"),
    )
    return jax.shard_map(
        functools.partial(shards, mesh.shape["ctx"]),
        mesh=mesh,
        in_specs=placed,
        out_specs=(P(("dp", "ctx"), "tp"), P(("dp", "ctx"), "tp")),
        check_vma=False,
    )
```

```python
import functools
import math

import jax
import jax.numpy as jnp
from jax import lax
from jax.experimental import pallas as pl
from jax.experimental.pallas import tpu as pltpu
from jax.sharding import PartitionSpec as P

P_DIM = 64
N_STATE = 256
KEY_DIM = 128
CHUNK = 256
RIM = 16
RIM_WIDTH = 384
EPS = 1e-05
NEG = -1e30
F32 = jnp.float32
BF16 = jnp.bfloat16


def dot(a, b):
    return jnp.dot(a, b, preferred_element_type=F32)


def dot_nt(a, b):
    return lax.dot_general(a, b, (((1,), (1,)), ((), ())), preferred_element_type=F32)


def silu(v):
    return v / (1.0 + jnp.exp(-v))


def log1p_unit(e):
    z = e / (2.0 + e)
    z2 = z * z
    acc = jnp.full_like(z, 1.0 / 17.0)
    for k in (15, 13, 11, 9, 7, 5, 3, 1):
        acc = acc * z2 + 1.0 / k
    return 2.0 * z * acc


def kernel(
    n,
    xbc_hbm,
    gate_hbm,
    dt_hbm,
    bias_hbm,
    alog_hbm,
    convw_hbm,
    convb_hbm,
    skip_hbm,
    gain_hbm,
    queries_hbm,
    keys_hbm,
    values_hbm,
    mamba_hbm,
    attn_hbm,
    mamba_out,
    attn_out,
    xbc,
    gate,
    dt_raw,
    dt_bias,
    a_log,
    conv_w,
    conv_b,
    skip,
    gain,
    queries,
    keys,
    values,
    rim_wide,
    rim_tall,
    rim_src,
    rim_dst,
    xc,
    kbuf,
    vbuf,
    dt_row,
    cum_row,
    skip_row,
    ecum_x,
    spread,
    s_own,
    h_in,
    h_out,
    r_in,
    r_out,
    c_next,
    y_acc,
    in_sems,
    mamba_sems,
    attn_sems,
    rim_send,
    rim_recv,
    k_send,
    k_recv,
    v_send,
    v_recv,
    h_send,
    h_recv,
    r_send,
    r_recv,
    c_send,
    c_recv,
):
    me = lax.axis_index("ctx")
    rows = xbc.shape[0]
    heads = dt_raw.shape[0]
    head_cols = heads * P_DIM
    groups = (xbc.shape[1] - head_cols) // (2 * N_STATE)
    per_group = heads // groups
    gcols = per_group * P_DIM
    per_chunks = gcols // CHUNK
    chunks = groups * per_chunks
    taps = conv_w.shape[0]
    kv_heads = keys.shape[1] // KEY_DIM
    repeat = queries.shape[1] // keys.shape[1]
    has_next = me < n - 1
    has_prev = me > 0
    right = me + 1
    is_last = me == n - 1
    before_last = me == n - 2
    pieces_wide = xbc.shape[1] // RIM_WIDTH

    pairs = (
        (xbc_hbm, xbc),
        (dt_hbm, dt_raw),
        (bias_hbm, dt_bias),
        (alog_hbm, a_log),
        (convw_hbm, conv_w),
        (convb_hbm, conv_b),
        (skip_hbm, skip),
        (keys_hbm, keys),
        (values_hbm, values),
        (queries_hbm, queries),
        (gate_hbm, gate),
        (gain_hbm, gain),
    )
    loads = [pltpu.make_async_copy(a, b, in_sems.at[i]) for i, (a, b) in enumerate(pairs)]
    for load in loads:
        load.start()

    def remote(src, dst, send, recv, to):
        return pltpu.make_async_remote_copy(
            src_ref=src,
            dst_ref=dst,
            send_sem=send,
            recv_sem=recv,
            device_id={"ctx": to},
            device_id_type=pl.DeviceIdType.MESH,
        )

    barrier = pltpu.get_barrier_semaphore()

    @pl.when(has_prev)
    def _():
        pl.semaphore_signal(
            barrier, inc=1, device_id={"ctx": me - 1}, device_id_type=pl.DeviceIdType.MESH
        )

    @pl.when((me >= 2) & has_next)
    def _():
        pl.semaphore_signal(
            barrier, inc=1, device_id={"ctx": me + 1}, device_id_type=pl.DeviceIdType.MESH
        )

    @pl.when(is_last)
    def _():
        pl.semaphore_signal(
            barrier, inc=1, device_id={"ctx": 0}, device_id_type=pl.DeviceIdType.MESH
        )

    def rim_copy():
        return remote(rim_src, rim_dst, rim_send, rim_recv, right)

    def own_kv():
        return (
            remote(keys_hbm, kbuf.at[me], k_send.at[me], k_recv.at[me], right),
            remote(values_hbm, vbuf.at[me], v_send.at[me], v_recv.at[me], right),
        )

    def kv_copy(block):
        return (
            remote(kbuf.at[block], kbuf.at[block], k_send.at[block], k_recv.at[block], right),
            remote(vbuf.at[block], vbuf.at[block], v_send.at[block], v_recv.at[block], right),
        )

    def far_kv():
        return (
            remote(keys_hbm, kbuf.at[0], k_send.at[n], k_recv.at[0], n - 1),
            remote(values_hbm, vbuf.at[0], v_send.at[n], v_recv.at[0], n - 1),
        )

    def back_kv():
        return (
            remote(kbuf.at[0], kbuf.at[0], k_send.at[0], k_recv.at[0], me - 1),
            remote(vbuf.at[0], vbuf.at[0], v_send.at[0], v_recv.at[0], me - 1),
        )

    def h_copy(c):
        return remote(h_out.at[c], h_in.at[c], h_send.at[c], h_recv.at[c], right)

    def r_copy(c):
        return remote(r_out.at[c], r_in.at[c], r_send.at[c], r_recv.at[c], right)

    def c_copy():
        return remote(
            xc.at[:, pl.ds(head_cols + groups * N_STATE, groups * N_STATE)],
            c_next,
            c_send,
            c_recv,
            me - 1,
        )

    @pl.when((me == 0) | ((me >= 3) & has_next))
    def _():
        pl.semaphore_wait(barrier, 2)

    @pl.when((me == 1) | (me == 2) | is_last)
    def _():
        pl.semaphore_wait(barrier, 1)

    loads[0].wait()

    @pl.when(has_next)
    def _():
        last = xbc[rows - RIM :, :].astype(F32)
        for p in range(pieces_wide):
            rim_tall[p * 3 : p * 3 + 3, :] = last[
                RIM - 3 :, p * RIM_WIDTH : (p + 1) * RIM_WIDTH
            ]
        rim_src[...] = rim_tall[...].astype(BF16)
        rim_copy().start()
        for copy in own_kv():
            copy.start()

        @pl.when(me == 0)
        def _():
            for copy in far_kv():
                copy.start()

    def clear(j, carry):
        @pl.when(j > me)
        def _():
            kbuf[j] = jnp.zeros(keys.shape, BF16)
            vbuf[j] = jnp.zeros(values.shape, BF16)

        return carry

    lax.fori_loop(0, n, clear, 0)
    for load in loads[1:7]:
        load.wait()

    def column(ref):
        return jnp.transpose(jnp.broadcast_to(ref[...], (rows, heads)))

    pre = dt_raw[...] + column(dt_bias)
    dt = jnp.maximum(pre, 0.0) + log1p_unit(jnp.exp(-jnp.abs(pre)))
    cum = -dt * jnp.exp(column(a_log))
    lane = lax.broadcasted_iota(jnp.int32, (heads, rows), 1)
    step = 1
    while step < rows:
        cum = cum + jnp.where(lane >= step, pltpu.roll(cum, step, 1), 0.0)
        step *= 2
    skip_row[...] = column(skip)
    dt_row[...] = dt
    cum_row[...] = cum
    spread_row = lax.broadcasted_iota(jnp.int32, (3 * per_group, gcols), 0)
    spread_col = lax.broadcasted_iota(jnp.int32, (3 * per_group, gcols), 1)
    hit = lax.rem(spread_row, per_group) == spread_col // P_DIM
    spread[...] = jnp.where(hit, 1.0, 0.0).astype(BF16)

    def expand(v):
        hi = v.astype(BF16).astype(F32)
        rest = v - hi
        mid = rest.astype(BF16).astype(F32)
        low = rest - mid
        parts = jnp.transpose(jnp.concatenate([hi, mid, low], axis=0))
        return dot(parts.astype(BF16), spread[...])

    rim_wide[...] = jnp.zeros(rim_wide.shape, F32)

    @pl.when(has_prev)
    def _():
        rim_copy().wait_recv()
        rim_tall[...] = rim_dst[...].astype(F32)
        for p in range(pieces_wide):
            rim_wide[5:, p * RIM_WIDTH : (p + 1) * RIM_WIDTH] = rim_tall[p * 3 : p * 3 + 3, :]

    def conv_tile(start, width):
        cols = pl.ds(pl.multiple_of(start, 256), width)
        ext = jnp.concatenate([rim_wide[:, cols], xbc[:, cols].astype(F32)], axis=0)
        acc = jnp.broadcast_to(conv_b[:, cols], (rows, width))
        for tap in range(taps):
            by = taps - 1 - tap
            moved = ext if by == 0 else pltpu.roll(ext, by, 0)
            acc = acc + conv_w[tap : tap + 1, cols] * moved[8:]
        out = silu(acc)
        xc[:, cols] = out.astype(BF16)
        return out

    def relay(s):
        block = me - 1 - s

        @pl.when((block >= 1) | ((block == 0) & (me == 1)))
        def _():
            for copy in kv_copy(block):
                copy.wait_recv()

            @pl.when(has_next & (block >= 1))
            def _():
                for copy in kv_copy(block):
                    copy.start()

    def group_rows(g):
        return pl.ds(pl.multiple_of(g * per_group, per_group), per_group)

    def first(g, carry):
        b_part = conv_tile(head_cols + g * N_STATE, N_STATE)
        b_turned = jnp.transpose(b_part).astype(BF16)
        cum_g = cum_row[group_rows(g), :]
        dt_g = dt_row[group_rows(g), :]
        last = jnp.broadcast_to(cum_g[:, rows - 1 :], cum_g.shape)
        tail = expand(dt_g * jnp.exp(last - cum_g))
        for i in range(per_chunks):
            c = g * per_chunks + i
            x_part = conv_tile(c * CHUNK, CHUNK).astype(BF16).astype(F32)
            weighted = (x_part * tail[:, i * CHUNK : (i + 1) * CHUNK]).astype(BF16)
            own = dot(b_turned, weighted)
            s_own[c] = own

            @pl.when(me == 0)
            def _():
                h_out[c] = own.astype(BF16)
                h_copy(c).start()

        ecum_x[:, pl.ds(pl.multiple_of(g * gcols, gcols), gcols)] = expand(jnp.exp(cum_g))
        conv_tile(head_cols + (groups + g) * N_STATE, N_STATE)

        @pl.when(g == max(groups - 2, 0))
        def _():
            relay(0)

        return carry

    lax.fori_loop(0, groups, first, 0)

    @pl.when(is_last)
    def _():
        c_copy().start()

    @pl.when(me >= 3)
    def _():
        for copy in back_kv():
            copy.wait_recv()
        for copy in back_kv():
            copy.start()

    def wait_third():
        @pl.when(me == 2)
        def _():
            for copy in back_kv():
                copy.wait_recv()

    for load in loads[7:]:
        load.wait()
    kbuf[me] = keys[...]
    vbuf[me] = values[...]

    def within(g):
        b_part = xc[:, pl.ds(pl.multiple_of(head_cols + g * N_STATE, N_STATE), N_STATE)]
        c_part = xc[:, pl.ds(pl.multiple_of(head_cols + (groups + g) * N_STATE, N_STATE), N_STATE)]
        products = dot_nt(c_part, b_part)
        cum_g = cum_row[group_rows(g), :]
        dt_g = dt_row[group_rows(g), :]
        skip_g = skip_row[group_rows(g), :]
        cum_t = jnp.transpose(cum_g)
        t_pos = lax.broadcasted_iota(jnp.int32, (rows, rows), 0)
        s_pos = lax.broadcasted_iota(jnp.int32, (rows, rows), 1)
        causal = s_pos <= t_pos
        low_half = lax.broadcasted_iota(jnp.int32, (rows, 2 * P_DIM), 1) < P_DIM
        for pair in range(per_group // 2):
            mixes = []
            for j in (2 * pair, 2 * pair + 1):
                gap = cum_t[:, j : j + 1] - cum_g[j : j + 1, :]
                decay = jnp.exp(jnp.where(causal, gap, NEG))
                mixes.append((products * decay * dt_g[j : j + 1, :]).astype(BF16))
            cols = pl.ds(pl.multiple_of(g * gcols + pair * 2 * P_DIM, 2 * P_DIM), 2 * P_DIM)
            x_pair = xc[:, cols].astype(F32)
            x_two = jnp.concatenate(
                [jnp.where(low_half, x_pair, 0.0), jnp.where(low_half, 0.0, x_pair)], axis=0
            ).astype(BF16)
            scale = jnp.where(
                low_half[:1], skip_g[2 * pair : 2 * pair + 1], skip_g[2 * pair + 1 : 2 * pair + 2]
            )
            y_acc[:, cols] = dot(jnp.concatenate(mixes, axis=1), x_two) + scale * x_pair

    pieces = kv_heads * 2
    piece_heads = repeat // 2
    log2_scale = 1.4426950408889634 / math.sqrt(KEY_DIM)

    def attn_flush(piece):
        width = piece_heads * KEY_DIM
        cols = pl.ds(pl.multiple_of(piece * width, width), width)
        return pltpu.make_async_copy(
            attn_out.at[:, cols], attn_hbm.at[:, cols], attn_sems.at[piece]
        )

    def attend(piece):
        kv_cols = pl.ds(pl.multiple_of((piece // 2) * KEY_DIM, KEY_DIM), KEY_DIM)
        k_all = jnp.concatenate([kbuf[j, :, kv_cols] for j in range(n)], axis=0)
        v_all = jnp.concatenate([vbuf[j, :, kv_cols] for j in range(n)], axis=0)
        q_pos = me * rows + lax.broadcasted_iota(jnp.int32, (rows, n * rows), 0)
        k_pos = lax.broadcasted_iota(jnp.int32, (rows, n * rows), 1)
        allowed = k_pos <= q_pos
        for j in range(piece_heads):
            start = (piece * piece_heads + j) * KEY_DIM
            cols = pl.ds(pl.multiple_of(start, KEY_DIM), KEY_DIM)
            scores = jnp.where(allowed, dot_nt(queries[:, cols], k_all), NEG)
            top = jnp.max(scores, axis=1, keepdims=True)
            probs = jnp.exp2((scores - top) * log2_scale)
            total = jnp.sum(probs, axis=1, keepdims=True)
            attn_out[:, cols] = (dot(probs.astype(BF16), v_all) / total).astype(BF16)
        attn_flush(piece).start()

    def mamba_flush(g):
        cols = pl.ds(pl.multiple_of(g * gcols, gcols), gcols)
        return pltpu.make_async_copy(
            mamba_out.at[:, cols], mamba_hbm.at[:, cols], mamba_sems.at[g]
        )

    def finish(g):
        cols = pl.ds(pl.multiple_of(g * gcols, gcols), gcols)
        v = y_acc[:, cols] * silu(gate[:, cols].astype(F32))
        scale = lax.rsqrt(jnp.mean(v * v, axis=1, keepdims=True) + EPS)
        mamba_out[:, cols] = (v * scale * gain[:, cols]).astype(BF16)
        mamba_flush(g).start()

    def chain(c, carry):
        g = c // per_chunks
        cols = pl.ds(pl.multiple_of(c * CHUNK, CHUNK), CHUNK)
        c_cols = pl.ds(pl.multiple_of(head_cols + (groups + g) * N_STATE, N_STATE), N_STATE)
        n_cols = pl.ds(pl.multiple_of(g * N_STATE, N_STATE), N_STATE)

        @pl.when((c >= 1) & (c < n - 1))
        def _():
            relay(c)

        def passed():
            total = ecum_x[rows - 1 : rows, cols]
            return (total * h_in[c].astype(F32) + s_own[c]).astype(BF16)

        @pl.when(has_prev & has_next)
        def _():
            h_copy(c).wait_recv()

        @pl.when(has_prev & (me < n - 2))
        def _():
            h_out[c] = passed()
            h_copy(c).start()

        @pl.when(before_last)
        def _():
            @pl.when(c == 0)
            def _():
                c_copy().wait_recv()

            r_out[c] = dot(c_next[:, n_cols], passed()).astype(BF16)
            r_copy(c).start()

        @pl.when(c < groups)
        def _():
            within(c)

        @pl.when(has_prev & has_next)
        def _():
            y_acc[:, cols] += ecum_x[:, cols] * dot(xc[:, c_cols], h_in[c])

        @pl.when(is_last)
        def _():
            r_copy(c).wait_recv()
            y_acc[:, cols] += ecum_x[:, cols] * r_in[c].astype(F32)

        @pl.when(lax.rem(c, per_chunks) == per_chunks - 1)
        def _():
            finish(g)

        @pl.when(c == lead)
        def _():
            wait_third()

        piece = c - lead

        @pl.when((piece >= 0) & (piece < pieces))
        def _():
            attend(piece)

        return carry

    lead = max(n - 1, groups)
    lax.fori_loop(0, chunks, chain, 0)
    for s in range(max(chunks, 1), n - 1):
        relay(s)

    def rest(piece, carry):
        attend(piece)
        return carry

    if chunks <= lead:
        wait_third()
    if chunks - lead < pieces:
        lax.fori_loop(max(chunks - lead, 0), pieces, rest, 0)

    @pl.when(has_next)
    def _():
        rim_copy().wait_send()
        for copy in own_kv():
            copy.wait_send()

        def sent_kv(block, carry):
            @pl.when((block >= 1) & (block < me))
            def _():
                for copy in kv_copy(block):
                    copy.wait_send()

            return carry

        lax.fori_loop(0, n, sent_kv, 0)

    def sent_h(c, carry):
        h_copy(c).wait_send()
        return carry

    def sent_r(c, carry):
        r_copy(c).wait_send()
        return carry

    @pl.when(me < n - 2)
    def _():
        lax.fori_loop(0, chunks, sent_h, 0)

    @pl.when(before_last)
    def _():
        lax.fori_loop(0, chunks, sent_r, 0)

    @pl.when(is_last)
    def _():
        c_copy().wait_send()

    @pl.when(me >= 3)
    def _():
        for copy in back_kv():
            copy.wait_send()

    @pl.when(me == 0)
    def _():
        for copy in far_kv():
            copy.wait_send()

    def out_done(g, carry):
        mamba_flush(g).wait()
        return carry

    def attn_done(piece, carry):
        attn_flush(piece).wait()
        return carry

    lax.fori_loop(0, pieces, attn_done, 0)
    lax.fori_loop(0, groups, out_done, 0)


def shards(
    n,
    xbc,
    gate_in,
    dt_raw,
    dt_bias,
    a_log,
    conv_weight,
    conv_bias,
    skip_weight,
    norm_gain,
    queries,
    keys,
    values,
):
    rows = xbc.shape[0]
    heads = dt_raw.shape[0]
    head_cols = heads * P_DIM
    groups = (xbc.shape[1] - head_cols) // (2 * N_STATE)
    per_group = heads // groups
    chunks = head_cols // CHUNK
    hbm = pl.BlockSpec(memory_space=pltpu.HBM)
    dma = pltpu.SemaphoreType.DMA
    args = (
        xbc,
        gate_in,
        dt_raw,
        dt_bias.reshape(1, -1),
        a_log.reshape(1, -1),
        conv_weight,
        conv_bias.reshape(1, -1),
        skip_weight.reshape(1, -1),
        norm_gain.reshape(1, -1),
        queries,
        keys,
        values,
    )
    rim_rows = -(-(3 * (xbc.shape[1] // RIM_WIDTH)) // RIM) * RIM
    return pl.pallas_call(
        functools.partial(kernel, n),
        out_shape=(
            jax.ShapeDtypeStruct((rows, head_cols), BF16),
            jax.ShapeDtypeStruct(queries.shape, BF16),
        ),
        in_specs=[hbm] * len(args),
        out_specs=(hbm, hbm),
        scratch_shapes=[
            pltpu.VMEM((rows, head_cols), BF16),
            pltpu.VMEM(queries.shape, BF16),
        ]
        + [pltpu.VMEM(a.shape, a.dtype) for a in args]
        + [
            pltpu.VMEM((8, xbc.shape[1]), F32),
            pltpu.VMEM((rim_rows, RIM_WIDTH), F32),
            pltpu.VMEM((rim_rows, RIM_WIDTH), BF16),
            pltpu.VMEM((rim_rows, RIM_WIDTH), BF16),
            pltpu.VMEM(xbc.shape, BF16),
            pltpu.VMEM((n,) + keys.shape, BF16),
            pltpu.VMEM((n,) + values.shape, BF16),
            pltpu.VMEM(dt_raw.shape, F32),
            pltpu.VMEM(dt_raw.shape, F32),
            pltpu.VMEM(dt_raw.shape, F32),
            pltpu.VMEM((rows, head_cols), F32),
            pltpu.VMEM((3 * per_group, per_group * P_DIM), BF16),
            pltpu.VMEM((chunks, N_STATE, CHUNK), F32),
            pltpu.VMEM((chunks, N_STATE, CHUNK), BF16),
            pltpu.VMEM((chunks, N_STATE, CHUNK), BF16),
            pltpu.VMEM((chunks, rows, CHUNK), BF16),
            pltpu.VMEM((chunks, rows, CHUNK), BF16),
            pltpu.VMEM((rows, groups * N_STATE), BF16),
            pltpu.VMEM((rows, head_cols), F32),
            dma((len(args),)),
            dma((groups,)),
            dma((2 * keys.shape[1] // KEY_DIM,)),
            dma,
            dma,
            dma((n + 1,)),
            dma((n,)),
            dma((n + 1,)),
            dma((n,)),
            dma((chunks,)),
            dma((chunks,)),
            dma((chunks,)),
            dma((chunks,)),
            dma,
            dma,
        ],
        compiler_params=pltpu.CompilerParams(
            collective_id=0, has_side_effects=True, vmem_limit_bytes=63 * 1024 * 1024
        ),
        name="mixers",
    )(*args)


def solution(mesh):
    placed = (
        P(("dp", "ctx"), "tp"),
        P(("dp", "ctx"), "tp"),
        P("tp", ("dp", "ctx")),
        P(("dp", "tp")),
        P("tp"),
        P(None, "tp"),
        P("tp"),
        P("tp"),
        P("tp"),
        P(("dp", "ctx"), "tp"),
        P(("dp", "ctx"), "tp"),
        P(("dp", "ctx"), "tp"),
    )
    return jax.shard_map(
        functools.partial(shards, mesh.shape["ctx"]),
        mesh=mesh,
        in_specs=placed,
        out_specs=(P(("dp", "ctx"), "tp"), P(("dp", "ctx"), "tp")),
        check_vma=False,
    )
```

```python
import functools
import math

import jax
import jax.numpy as jnp
from jax import lax
from jax.experimental import pallas as pl
from jax.experimental.pallas import tpu as pltpu
from jax.sharding import PartitionSpec as P

P_DIM = 64
N_STATE = 256
KEY_DIM = 128
CHUNK = 256
RIM = 16
RIM_WIDTH = 384
VMEM_BYTES = 63 * 1024 * 1024
EPS = 1e-05
NEG = -1e30
F32 = jnp.float32
BF16 = jnp.bfloat16


def dot(a, b):
    return jnp.dot(a, b, preferred_element_type=F32)


def dot_nt(a, b):
    return lax.dot_general(a, b, (((1,), (1,)), ((), ())), preferred_element_type=F32)


def silu(v):
    return v / (1.0 + jnp.exp(-v))


def log1p_unit(e):
    z = e / (2.0 + e)
    z2 = z * z
    acc = jnp.full_like(z, 1.0 / 17.0)
    for k in (15, 13, 11, 9, 7, 5, 3, 1):
        acc = acc * z2 + 1.0 / k
    return 2.0 * z * acc


def kernel(
    n,
    xbc_hbm,
    gate_hbm,
    dt_hbm,
    bias_hbm,
    alog_hbm,
    convw_hbm,
    convb_hbm,
    skip_hbm,
    gain_hbm,
    queries_hbm,
    keys_hbm,
    values_hbm,
    mamba_hbm,
    attn_hbm,
    mamba_out,
    attn_out,
    xbc,
    gate,
    dt_raw,
    dt_bias,
    a_log,
    conv_w,
    conv_b,
    skip,
    gain,
    queries,
    keys,
    values,
    xbc_last,
    rim_wide,
    rim_tall,
    rim_src,
    rim_dst,
    xc,
    kbuf,
    vbuf,
    dt_row,
    cum_row,
    skip_row,
    ecum_x,
    spread,
    s_own,
    h_in,
    h_out,
    r_in,
    r_out,
    c_next,
    y_acc,
    in_sems,
    mamba_sems,
    attn_sems,
    rim_send,
    rim_recv,
    k_send,
    k_recv,
    v_send,
    v_recv,
    h_send,
    h_recv,
    r_send,
    r_recv,
    c_send,
    c_recv,
):
    me = lax.axis_index("ctx")
    rows = xbc.shape[0]
    heads = dt_raw.shape[0]
    head_cols = heads * P_DIM
    groups = (xbc.shape[1] - head_cols) // (2 * N_STATE)
    per_group = heads // groups
    gcols = per_group * P_DIM
    per_chunks = gcols // CHUNK
    chunks = groups * per_chunks
    taps = conv_w.shape[0]
    kv_heads = keys.shape[1] // KEY_DIM
    repeat = queries.shape[1] // keys.shape[1]
    has_next = me < n - 1
    has_prev = me > 0
    right = me + 1
    is_last = me == n - 1
    before_last = me == n - 2
    pieces_wide = xbc.shape[1] // RIM_WIDTH

    pairs = (
        (xbc_hbm.at[pl.ds(rows - RIM, RIM), :], xbc_last),
        (xbc_hbm, xbc),
        (dt_hbm, dt_raw),
        (bias_hbm, dt_bias),
        (alog_hbm, a_log),
        (convw_hbm, conv_w),
        (convb_hbm, conv_b),
        (skip_hbm, skip),
        (keys_hbm, keys),
        (values_hbm, values),
        (queries_hbm, queries),
        (gate_hbm, gate),
        (gain_hbm, gain),
    )
    loads = [pltpu.make_async_copy(a, b, in_sems.at[i]) for i, (a, b) in enumerate(pairs)]
    for load in loads:
        load.start()

    def remote(src, dst, send, recv, to):
        return pltpu.make_async_remote_copy(
            src_ref=src,
            dst_ref=dst,
            send_sem=send,
            recv_sem=recv,
            device_id={"ctx": to},
            device_id_type=pl.DeviceIdType.MESH,
        )

    barrier = pltpu.get_barrier_semaphore()

    @pl.when(has_prev)
    def _():
        pl.semaphore_signal(
            barrier, inc=1, device_id={"ctx": me - 1}, device_id_type=pl.DeviceIdType.MESH
        )

    @pl.when(before_last)
    def _():
        pl.semaphore_signal(
            barrier, inc=1, device_id={"ctx": me + 1}, device_id_type=pl.DeviceIdType.MESH
        )

    def rim_copy():
        return remote(rim_src, rim_dst, rim_send, rim_recv, right)

    def own_k():
        return remote(keys_hbm, kbuf.at[me], k_send.at[me], k_recv.at[me], right)

    def own_v():
        return remote(values_hbm, vbuf.at[me], v_send.at[me], v_recv.at[me], right)

    def k_copy(block):
        return remote(kbuf.at[block], kbuf.at[block], k_send.at[block], k_recv.at[block], right)

    def v_copy(block):
        return remote(vbuf.at[block], vbuf.at[block], v_send.at[block], v_recv.at[block], right)

    def h_copy(c):
        return remote(h_out.at[c], h_in.at[c], h_send.at[c], h_recv.at[c], right)

    def r_copy(c):
        return remote(r_out.at[c], r_in.at[c], r_send.at[c], r_recv.at[c], right)

    def c_copy():
        return remote(
            xc.at[:, pl.ds(head_cols + groups * N_STATE, groups * N_STATE)],
            c_next,
            c_send,
            c_recv,
            me - 1,
        )

    pl.semaphore_wait(barrier, 1)
    loads[0].wait()

    @pl.when(has_next)
    def _():
        last = xbc_last[...].astype(F32)
        for p in range(pieces_wide):
            rim_tall[p * 3 : p * 3 + 3, :] = last[
                RIM - 3 :, p * RIM_WIDTH : (p + 1) * RIM_WIDTH
            ]
        rim_src[...] = rim_tall[...].astype(BF16)
        rim_copy().start()
        own_k().start()

        @pl.when(has_prev)
        def _():
            own_v().start()

    def clear(j, carry):
        @pl.when(j > me)
        def _():
            kbuf[j] = jnp.zeros(keys.shape, BF16)
            vbuf[j] = jnp.zeros(values.shape, BF16)

        return carry

    lax.fori_loop(0, n, clear, 0)
    for load in loads[1:8]:
        load.wait()

    def column(ref):
        return jnp.transpose(jnp.broadcast_to(ref[...], (rows, heads)))

    pre = dt_raw[...] + column(dt_bias)
    dt = jnp.maximum(pre, 0.0) + log1p_unit(jnp.exp(-jnp.abs(pre)))
    cum = -dt * jnp.exp(column(a_log))
    lane = lax.broadcasted_iota(jnp.int32, (heads, rows), 1)
    step = 1
    while step < rows:
        cum = cum + jnp.where(lane >= step, pltpu.roll(cum, step, 1), 0.0)
        step *= 2
    skip_row[...] = column(skip)
    dt_row[...] = dt
    cum_row[...] = cum
    spread_row = lax.broadcasted_iota(jnp.int32, (3 * per_group, gcols), 0)
    spread_col = lax.broadcasted_iota(jnp.int32, (3 * per_group, gcols), 1)
    hit = lax.rem(spread_row, per_group) == spread_col // P_DIM
    spread[...] = jnp.where(hit, 1.0, 0.0).astype(BF16)

    def expand(v):
        hi = v.astype(BF16).astype(F32)
        rest = v - hi
        mid = rest.astype(BF16).astype(F32)
        low = rest - mid
        parts = jnp.transpose(jnp.concatenate([hi, mid, low], axis=0))
        return dot(parts.astype(BF16), spread[...])

    rim_wide[...] = jnp.zeros(rim_wide.shape, F32)

    @pl.when(has_prev)
    def _():
        rim_copy().wait_recv()
        rim_tall[...] = rim_dst[...].astype(F32)
        for p in range(pieces_wide):
            rim_wide[5:, p * RIM_WIDTH : (p + 1) * RIM_WIDTH] = rim_tall[p * 3 : p * 3 + 3, :]

    def conv_tile(start, width):
        cols = pl.ds(pl.multiple_of(start, 256), width)
        ext = jnp.concatenate([rim_wide[:, cols], xbc[:, cols].astype(F32)], axis=0)
        acc = jnp.broadcast_to(conv_b[:, cols], (rows, width))
        for tap in range(taps):
            by = taps - 1 - tap
            moved = ext if by == 0 else pltpu.roll(ext, by, 0)
            acc = acc + conv_w[tap : tap + 1, cols] * moved[8:]
        out = silu(acc)
        xc[:, cols] = out.astype(BF16)
        return out

    def passing(copy, block):
        @pl.when((block >= 0) & (block < me))
        def _():
            copy(block).wait_recv()

            @pl.when(has_next)
            def _():
                copy(block).start()

    late = per_chunks

    def relay(c):
        block = me - 1 - c

        @pl.when(c >= 1)
        def _():
            passing(k_copy, block)

            @pl.when(block >= 1)
            def _():
                passing(v_copy, block)

        @pl.when((me >= 1) & (c == late + me - 1))
        def _():
            passing(v_copy, 0)

    def group_rows(g):
        return pl.ds(pl.multiple_of(g * per_group, per_group), per_group)

    def first(g, carry):
        b_part = conv_tile(head_cols + g * N_STATE, N_STATE)
        b_turned = jnp.transpose(b_part).astype(BF16)
        cum_g = cum_row[group_rows(g), :]
        dt_g = dt_row[group_rows(g), :]
        last = jnp.broadcast_to(cum_g[:, rows - 1 :], cum_g.shape)
        tail = expand(dt_g * jnp.exp(last - cum_g))
        for i in range(per_chunks):
            c = g * per_chunks + i
            x_part = conv_tile(c * CHUNK, CHUNK).astype(BF16).astype(F32)
            weighted = (x_part * tail[:, i * CHUNK : (i + 1) * CHUNK]).astype(BF16)
            own = dot(b_turned, weighted)
            s_own[c] = own

            @pl.when(me == 0)
            def _():
                h_out[c] = own.astype(BF16)
                h_copy(c).start()

        ecum_x[:, pl.ds(pl.multiple_of(g * gcols, gcols), gcols)] = expand(jnp.exp(cum_g))
        conv_tile(head_cols + (groups + g) * N_STATE, N_STATE)

        @pl.when((me == 0) & (g == 0))
        def _():
            own_v().start()

        @pl.when(g == min(1, groups - 1))
        def _():
            passing(k_copy, me - 1)

        @pl.when((g == groups - 1) & (me >= 2))
        def _():
            passing(v_copy, me - 1)

        return carry

    lax.fori_loop(0, groups, first, 0)

    @pl.when(is_last)
    def _():
        c_copy().start()

    for load in loads[8:]:
        load.wait()
    kbuf[me] = keys[...]
    vbuf[me] = values[...]

    def within(g):
        b_part = xc[:, pl.ds(pl.multiple_of(head_cols + g * N_STATE, N_STATE), N_STATE)]
        c_part = xc[:, pl.ds(pl.multiple_of(head_cols + (groups + g) * N_STATE, N_STATE), N_STATE)]
        products = dot_nt(c_part, b_part)
        cum_g = cum_row[group_rows(g), :]
        dt_g = dt_row[group_rows(g), :]
        skip_g = skip_row[group_rows(g), :]
        cum_t = jnp.transpose(cum_g)
        t_pos = lax.broadcasted_iota(jnp.int32, (rows, rows), 0)
        s_pos = lax.broadcasted_iota(jnp.int32, (rows, rows), 1)
        causal = s_pos <= t_pos
        low_half = lax.broadcasted_iota(jnp.int32, (rows, 2 * P_DIM), 1) < P_DIM
        for pair in range(per_group // 2):
            mixes = []
            for j in (2 * pair, 2 * pair + 1):
                gap = cum_t[:, j : j + 1] - cum_g[j : j + 1, :]
                decay = jnp.exp(jnp.where(causal, gap, NEG))
                mixes.append((products * decay * dt_g[j : j + 1, :]).astype(BF16))
            cols = pl.ds(pl.multiple_of(g * gcols + pair * 2 * P_DIM, 2 * P_DIM), 2 * P_DIM)
            x_pair = xc[:, cols].astype(F32)
            x_two = jnp.concatenate(
                [jnp.where(low_half, x_pair, 0.0), jnp.where(low_half, 0.0, x_pair)], axis=0
            ).astype(BF16)
            scale = jnp.where(
                low_half[:1], skip_g[2 * pair : 2 * pair + 1], skip_g[2 * pair + 1 : 2 * pair + 2]
            )
            y_acc[:, cols] = dot(jnp.concatenate(mixes, axis=1), x_two) + scale * x_pair

    pieces = kv_heads * 2
    piece_heads = repeat // 2
    log2_scale = 1.4426950408889634 / math.sqrt(KEY_DIM)

    def attn_flush(piece):
        width = piece_heads * KEY_DIM
        cols = pl.ds(pl.multiple_of(piece * width, width), width)
        return pltpu.make_async_copy(
            attn_out.at[:, cols], attn_hbm.at[:, cols], attn_sems.at[piece]
        )

    def attend(piece):
        kv_cols = pl.ds(pl.multiple_of((piece // 2) * KEY_DIM, KEY_DIM), KEY_DIM)
        k_all = jnp.concatenate([kbuf[j, :, kv_cols] for j in range(n)], axis=0)
        v_all = jnp.concatenate([vbuf[j, :, kv_cols] for j in range(n)], axis=0)
        q_pos = me * rows + lax.broadcasted_iota(jnp.int32, (rows, n * rows), 0)
        k_pos = lax.broadcasted_iota(jnp.int32, (rows, n * rows), 1)
        allowed = k_pos <= q_pos
        for j in range(piece_heads):
            start = (piece * piece_heads + j) * KEY_DIM
            cols = pl.ds(pl.multiple_of(start, KEY_DIM), KEY_DIM)
            scores = jnp.where(allowed, dot_nt(queries[:, cols], k_all), NEG)
            top = jnp.max(scores, axis=1, keepdims=True)
            probs = jnp.exp2((scores - top) * log2_scale)
            total = jnp.sum(probs, axis=1, keepdims=True)
            attn_out[:, cols] = (dot(probs.astype(BF16), v_all) / total).astype(BF16)
        attn_flush(piece).start()

    def mamba_flush(g):
        cols = pl.ds(pl.multiple_of(g * gcols, gcols), gcols)
        return pltpu.make_async_copy(
            mamba_out.at[:, cols], mamba_hbm.at[:, cols], mamba_sems.at[g]
        )

    def finish(g):
        cols = pl.ds(pl.multiple_of(g * gcols, gcols), gcols)
        v = y_acc[:, cols] * silu(gate[:, cols].astype(F32))
        scale = lax.rsqrt(jnp.mean(v * v, axis=1, keepdims=True) + EPS)
        mamba_out[:, cols] = (v * scale * gain[:, cols]).astype(BF16)
        mamba_flush(g).start()

    def chain(c, carry):
        g = c // per_chunks
        cols = pl.ds(pl.multiple_of(c * CHUNK, CHUNK), CHUNK)
        c_cols = pl.ds(pl.multiple_of(head_cols + (groups + g) * N_STATE, N_STATE), N_STATE)
        n_cols = pl.ds(pl.multiple_of(g * N_STATE, N_STATE), N_STATE)

        relay(c)

        def passed():
            total = ecum_x[rows - 1 : rows, cols]
            return (total * h_in[c].astype(F32) + s_own[c]).astype(BF16)

        @pl.when(has_prev & has_next)
        def _():
            h_copy(c).wait_recv()

        @pl.when(has_prev & (me < n - 2))
        def _():
            h_out[c] = passed()
            h_copy(c).start()

        @pl.when(before_last)
        def _():
            @pl.when(c == 0)
            def _():
                c_copy().wait_recv()

            r_out[c] = dot(c_next[:, n_cols], passed()).astype(BF16)
            r_copy(c).start()

        @pl.when(c < groups)
        def _():
            within(c)

        @pl.when(has_prev & has_next)
        def _():
            y_acc[:, cols] += ecum_x[:, cols] * dot(xc[:, c_cols], h_in[c])

        @pl.when(is_last)
        def _():
            r_copy(c).wait_recv()
            y_acc[:, cols] += ecum_x[:, cols] * r_in[c].astype(F32)

        @pl.when(lax.rem(c, per_chunks) == per_chunks - 1)
        def _():
            finish(g)

        piece = c - lead

        @pl.when((piece >= 0) & (piece < pieces))
        def _():
            attend(piece)

        return carry

    lead = max(late + n - 1, groups)
    lax.fori_loop(0, chunks, chain, 0)
    for c in range(chunks, late + n - 1):
        relay(c)

    def rest(piece, carry):
        attend(piece)
        return carry

    if chunks - lead < pieces:
        lax.fori_loop(max(chunks - lead, 0), pieces, rest, 0)

    @pl.when(has_next)
    def _():
        rim_copy().wait_send()
        own_k().wait_send()
        own_v().wait_send()

        def sent_kv(block, carry):
            @pl.when(block < me)
            def _():
                k_copy(block).wait_send()
                v_copy(block).wait_send()

            return carry

        lax.fori_loop(0, n, sent_kv, 0)

    def sent_h(c, carry):
        h_copy(c).wait_send()
        return carry

    def sent_r(c, carry):
        r_copy(c).wait_send()
        return carry

    @pl.when(me < n - 2)
    def _():
        lax.fori_loop(0, chunks, sent_h, 0)

    @pl.when(before_last)
    def _():
        lax.fori_loop(0, chunks, sent_r, 0)

    @pl.when(is_last)
    def _():
        c_copy().wait_send()

    def out_done(g, carry):
        mamba_flush(g).wait()
        return carry

    def attn_done(piece, carry):
        attn_flush(piece).wait()
        return carry

    lax.fori_loop(0, pieces, attn_done, 0)
    lax.fori_loop(0, groups, out_done, 0)


def hand_on(mamba_src, attn_src, mamba_dst, attn_dst, sems):
    half = mamba_src.shape[0] // 2
    copies = []
    for i, (src, dst) in enumerate(((mamba_src, mamba_dst), (attn_src, attn_dst))):
        for j in range(2):
            part = pl.ds(j * half, half)
            copies.append(
                pltpu.make_async_copy(src.at[part, :], dst.at[part, :], sems.at[2 * i + j])
            )
    for copy in copies:
        copy.start()
    for copy in copies:
        copy.wait()


def shards(
    n,
    xbc,
    gate_in,
    dt_raw,
    dt_bias,
    a_log,
    conv_weight,
    conv_bias,
    skip_weight,
    norm_gain,
    queries,
    keys,
    values,
):
    rows = xbc.shape[0]
    heads = dt_raw.shape[0]
    head_cols = heads * P_DIM
    groups = (xbc.shape[1] - head_cols) // (2 * N_STATE)
    per_group = heads // groups
    chunks = head_cols // CHUNK
    hbm = pl.BlockSpec(memory_space=pltpu.HBM)
    dma = pltpu.SemaphoreType.DMA
    args = (
        xbc,
        gate_in,
        dt_raw,
        dt_bias.reshape(1, -1),
        a_log.reshape(1, -1),
        conv_weight,
        conv_bias.reshape(1, -1),
        skip_weight.reshape(1, -1),
        norm_gain.reshape(1, -1),
        queries,
        keys,
        values,
    )
    rim_rows = -(-(3 * (xbc.shape[1] // RIM_WIDTH)) // RIM) * RIM
    out_shape = (
        jax.ShapeDtypeStruct((rows, head_cols), BF16),
        jax.ShapeDtypeStruct(queries.shape, BF16),
    )
    outs = pl.pallas_call(
        functools.partial(kernel, n),
        out_shape=out_shape,
        in_specs=[hbm] * len(args),
        out_specs=(hbm, hbm),
        scratch_shapes=[
            pltpu.VMEM((rows, head_cols), BF16),
            pltpu.VMEM(queries.shape, BF16),
        ]
        + [pltpu.VMEM(a.shape, a.dtype) for a in args]
        + [
            pltpu.VMEM((RIM, xbc.shape[1]), BF16),
            pltpu.VMEM((8, xbc.shape[1]), F32),
            pltpu.VMEM((rim_rows, RIM_WIDTH), F32),
            pltpu.VMEM((rim_rows, RIM_WIDTH), BF16),
            pltpu.VMEM((rim_rows, RIM_WIDTH), BF16),
            pltpu.VMEM(xbc.shape, BF16),
            pltpu.VMEM((n,) + keys.shape, BF16),
            pltpu.VMEM((n,) + values.shape, BF16),
            pltpu.VMEM(dt_raw.shape, F32),
            pltpu.VMEM(dt_raw.shape, F32),
            pltpu.VMEM(dt_raw.shape, F32),
            pltpu.VMEM((rows, head_cols), F32),
            pltpu.VMEM((3 * per_group, per_group * P_DIM), BF16),
            pltpu.VMEM((chunks, N_STATE, CHUNK), F32),
            pltpu.VMEM((chunks, N_STATE, CHUNK), BF16),
            pltpu.VMEM((chunks, N_STATE, CHUNK), BF16),
            pltpu.VMEM((chunks, rows, CHUNK), BF16),
            pltpu.VMEM((chunks, rows, CHUNK), BF16),
            pltpu.VMEM((rows, groups * N_STATE), BF16),
            pltpu.VMEM((rows, head_cols), F32),
            dma((len(args) + 1,)),
            dma((groups,)),
            dma((2 * keys.shape[1] // KEY_DIM,)),
            dma,
            dma,
            dma((n,)),
            dma((n,)),
            dma((n,)),
            dma((n,)),
            dma((chunks,)),
            dma((chunks,)),
            dma((chunks,)),
            dma((chunks,)),
            dma,
            dma,
        ],
        compiler_params=pltpu.CompilerParams(
            collective_id=0, has_side_effects=True, vmem_limit_bytes=VMEM_BYTES
        ),
        name="mixers",
    )(*args)
    return pl.pallas_call(
        hand_on,
        out_shape=out_shape,
        in_specs=[hbm, hbm],
        out_specs=(hbm, hbm),
        scratch_shapes=[dma((4,))],
        compiler_params=pltpu.CompilerParams(vmem_limit_bytes=VMEM_BYTES),
        name="hand_on",
    )(*outs)


def solution(mesh):
    placed = (
        P(("dp", "ctx"), "tp"),
        P(("dp", "ctx"), "tp"),
        P("tp", ("dp", "ctx")),
        P(("dp", "tp")),
        P("tp"),
        P(None, "tp"),
        P("tp"),
        P("tp"),
        P("tp"),
        P(("dp", "ctx"), "tp"),
        P(("dp", "ctx"), "tp"),
        P(("dp", "ctx"), "tp"),
    )
    return jax.shard_map(
        functools.partial(shards, mesh.shape["ctx"]),
        mesh=mesh,
        in_specs=placed,
        out_specs=(P(("dp", "ctx"), "tp"), P(("dp", "ctx"), "tp")),
        check_vma=False,
    )
```

```python
import functools
import math

import jax
import jax.numpy as jnp
from jax import lax
from jax.experimental import pallas as pl
from jax.experimental.pallas import tpu as pltpu
from jax.sharding import PartitionSpec as P

P_DIM = 64
N_STATE = 256
KEY_DIM = 128
CHUNK = 128
TILE = 256
RIM = 16
RIM_WIDTH = 384
VMEM_BYTES = 63 * 1024 * 1024
EPS = 1e-05
NEG = -1e30
F32 = jnp.float32
BF16 = jnp.bfloat16


def dot(a, b):
    return jnp.dot(a, b, preferred_element_type=F32)


def dot_nt(a, b):
    return lax.dot_general(a, b, (((1,), (1,)), ((), ())), preferred_element_type=F32)


def silu(v):
    return v / (1.0 + jnp.exp(-v))


def log1p_unit(e):
    z = e / (2.0 + e)
    z2 = z * z
    acc = jnp.full_like(z, 1.0 / 17.0)
    for k in (15, 13, 11, 9, 7, 5, 3, 1):
        acc = acc * z2 + 1.0 / k
    return 2.0 * z * acc


def kernel(
    n,
    xbc_hbm,
    gate_hbm,
    dt_hbm,
    bias_hbm,
    alog_hbm,
    convw_hbm,
    convb_hbm,
    skip_hbm,
    gain_hbm,
    queries_hbm,
    keys_hbm,
    values_hbm,
    mamba_hbm,
    attn_hbm,
    mamba_out,
    attn_out,
    xbc,
    gate,
    dt_raw,
    dt_bias,
    a_log,
    conv_w,
    conv_b,
    skip,
    gain,
    queries,
    keys,
    values,
    xbc_last,
    rim_wide,
    rim_tall,
    rim_src,
    rim_dst,
    xc,
    kbuf,
    vbuf,
    dt_row,
    cum_row,
    skip_row,
    ecum_x,
    spread,
    s_own,
    h_in,
    h_out,
    r_in,
    r_out,
    c_next,
    y_acc,
    in_sems,
    mamba_sems,
    attn_sems,
    rim_send,
    rim_recv,
    k_send,
    k_recv,
    v_send,
    v_recv,
    h_send,
    h_recv,
    r_send,
    r_recv,
    c_send,
    c_recv,
):
    me = lax.axis_index("ctx")
    rows = xbc.shape[0]
    heads = dt_raw.shape[0]
    head_cols = heads * P_DIM
    groups = (xbc.shape[1] - head_cols) // (2 * N_STATE)
    per_group = heads // groups
    gcols = per_group * P_DIM
    per_chunks = gcols // CHUNK
    chunks = groups * per_chunks
    taps = conv_w.shape[0]
    kv_heads = keys.shape[1] // KEY_DIM
    repeat = queries.shape[1] // keys.shape[1]
    has_next = me < n - 1
    has_prev = me > 0
    right = me + 1
    is_last = me == n - 1
    before_last = me == n - 2
    pieces_wide = xbc.shape[1] // RIM_WIDTH

    pairs = (
        (xbc_hbm.at[pl.ds(rows - RIM, RIM), :], xbc_last),
        (xbc_hbm, xbc),
        (dt_hbm, dt_raw),
        (bias_hbm, dt_bias),
        (alog_hbm, a_log),
        (convw_hbm, conv_w),
        (convb_hbm, conv_b),
        (skip_hbm, skip),
        (keys_hbm, keys),
        (values_hbm, values),
        (queries_hbm, queries),
        (gate_hbm, gate),
        (gain_hbm, gain),
    )
    loads = [pltpu.make_async_copy(a, b, in_sems.at[i]) for i, (a, b) in enumerate(pairs)]
    for load in loads:
        load.start()

    def remote(src, dst, send, recv, to):
        return pltpu.make_async_remote_copy(
            src_ref=src,
            dst_ref=dst,
            send_sem=send,
            recv_sem=recv,
            device_id={"ctx": to},
            device_id_type=pl.DeviceIdType.MESH,
        )

    barrier = pltpu.get_barrier_semaphore()

    @pl.when(has_prev)
    def _():
        pl.semaphore_signal(
            barrier, inc=1, device_id={"ctx": me - 1}, device_id_type=pl.DeviceIdType.MESH
        )

    @pl.when(before_last)
    def _():
        pl.semaphore_signal(
            barrier, inc=1, device_id={"ctx": me + 1}, device_id_type=pl.DeviceIdType.MESH
        )

    def rim_copy():
        return remote(rim_src, rim_dst, rim_send, rim_recv, right)

    def own_k():
        return remote(keys_hbm, kbuf.at[me], k_send.at[me], k_recv.at[me], right)

    def own_v():
        return remote(values_hbm, vbuf.at[me], v_send.at[me], v_recv.at[me], right)

    def k_copy(block):
        return remote(kbuf.at[block], kbuf.at[block], k_send.at[block], k_recv.at[block], right)

    def v_copy(block):
        return remote(vbuf.at[block], vbuf.at[block], v_send.at[block], v_recv.at[block], right)

    def h_copy(c):
        return remote(h_out.at[c], h_in.at[c], h_send.at[c], h_recv.at[c], right)

    def r_copy(c):
        return remote(r_out.at[c], r_in.at[c], r_send.at[c], r_recv.at[c], right)

    def c_copy():
        return remote(
            xc.at[:, pl.ds(head_cols + groups * N_STATE, groups * N_STATE)],
            c_next,
            c_send,
            c_recv,
            me - 1,
        )

    pl.semaphore_wait(barrier, 1)
    loads[0].wait()

    @pl.when(has_next)
    def _():
        last = xbc_last[...].astype(F32)
        for p in range(pieces_wide):
            rim_tall[p * 3 : p * 3 + 3, :] = last[
                RIM - 3 :, p * RIM_WIDTH : (p + 1) * RIM_WIDTH
            ]
        rim_src[...] = rim_tall[...].astype(BF16)
        rim_copy().start()
        own_k().start()

        @pl.when(has_prev)
        def _():
            own_v().start()

    def clear(j, carry):
        @pl.when(j > me)
        def _():
            kbuf[j] = jnp.zeros(keys.shape, BF16)
            vbuf[j] = jnp.zeros(values.shape, BF16)

        return carry

    lax.fori_loop(0, n, clear, 0)
    for load in loads[1:8]:
        load.wait()

    def column(ref):
        return jnp.transpose(jnp.broadcast_to(ref[...], (rows, heads)))

    pre = dt_raw[...] + column(dt_bias)
    dt = jnp.maximum(pre, 0.0) + log1p_unit(jnp.exp(-jnp.abs(pre)))
    cum = -dt * jnp.exp(column(a_log))
    lane = lax.broadcasted_iota(jnp.int32, (heads, rows), 1)
    step = 1
    while step < rows:
        cum = cum + jnp.where(lane >= step, pltpu.roll(cum, step, 1), 0.0)
        step *= 2
    skip_row[...] = column(skip)
    dt_row[...] = dt
    cum_row[...] = cum
    spread_row = lax.broadcasted_iota(jnp.int32, (3 * per_group, gcols), 0)
    spread_col = lax.broadcasted_iota(jnp.int32, (3 * per_group, gcols), 1)
    hit = lax.rem(spread_row, per_group) == spread_col // P_DIM
    spread[...] = jnp.where(hit, 1.0, 0.0).astype(BF16)

    def expand(v):
        hi = v.astype(BF16).astype(F32)
        rest = v - hi
        mid = rest.astype(BF16).astype(F32)
        low = rest - mid
        parts = jnp.transpose(jnp.concatenate([hi, mid, low], axis=0))
        return dot(parts.astype(BF16), spread[...])

    rim_wide[...] = jnp.zeros(rim_wide.shape, F32)

    @pl.when(has_prev)
    def _():
        rim_copy().wait_recv()
        rim_tall[...] = rim_dst[...].astype(F32)
        for p in range(pieces_wide):
            rim_wide[5:, p * RIM_WIDTH : (p + 1) * RIM_WIDTH] = rim_tall[p * 3 : p * 3 + 3, :]

    def conv_tile(start, width):
        cols = pl.ds(pl.multiple_of(start, 256), width)
        ext = jnp.concatenate([rim_wide[:, cols], xbc[:, cols].astype(F32)], axis=0)
        acc = jnp.broadcast_to(conv_b[:, cols], (rows, width))
        for tap in range(taps):
            by = taps - 1 - tap
            moved = ext if by == 0 else pltpu.roll(ext, by, 0)
            acc = acc + conv_w[tap : tap + 1, cols] * moved[8:]
        out = silu(acc)
        xc[:, cols] = out.astype(BF16)
        return out

    def passing(copy, block):
        @pl.when((block >= 0) & (block < me))
        def _():
            copy(block).wait_recv()

            @pl.when(has_next)
            def _():
                copy(block).start()

    late = per_chunks

    def relay(c):
        block = me - 1 - c

        @pl.when(c >= 1)
        def _():
            passing(k_copy, block)

            @pl.when(block >= 1)
            def _():
                passing(v_copy, block)

        @pl.when((me >= 1) & (c == late + me - 1))
        def _():
            passing(v_copy, 0)

    def group_rows(g):
        return pl.ds(pl.multiple_of(g * per_group, per_group), per_group)

    def first(g, carry):
        b_part = conv_tile(head_cols + g * N_STATE, N_STATE)
        b_turned = jnp.transpose(b_part).astype(BF16)
        cum_g = cum_row[group_rows(g), :]
        dt_g = dt_row[group_rows(g), :]
        last = jnp.broadcast_to(cum_g[:, rows - 1 :], cum_g.shape)
        tail = expand(dt_g * jnp.exp(last - cum_g))
        for i in range(gcols // TILE):
            x_part = conv_tile(g * gcols + i * TILE, TILE).astype(BF16).astype(F32)
            weighted = (x_part * tail[:, i * TILE : (i + 1) * TILE]).astype(BF16)
            own = dot(b_turned, weighted)
            for j in range(TILE // CHUNK):
                c = g * per_chunks + i * (TILE // CHUNK) + j
                s_own[c] = own[:, j * CHUNK : (j + 1) * CHUNK]

            @pl.when(me == 0)
            def _():
                for j in range(TILE // CHUNK):
                    c = g * per_chunks + i * (TILE // CHUNK) + j
                    h_out[c] = own[:, j * CHUNK : (j + 1) * CHUNK].astype(BF16)
                    h_copy(c).start()

        ecum_x[:, pl.ds(pl.multiple_of(g * gcols, gcols), gcols)] = expand(jnp.exp(cum_g))
        conv_tile(head_cols + (groups + g) * N_STATE, N_STATE)

        @pl.when((me == 0) & (g == 0))
        def _():
            own_v().start()

        @pl.when(g == min(1, groups - 1))
        def _():
            passing(k_copy, me - 1)

        @pl.when((g == groups - 1) & (me >= 2))
        def _():
            passing(v_copy, me - 1)

        return carry

    lax.fori_loop(0, groups, first, 0)

    @pl.when(is_last)
    def _():
        c_copy().start()

    for load in loads[8:]:
        load.wait()
    kbuf[me] = keys[...]
    vbuf[me] = values[...]

    def within(g):
        b_part = xc[:, pl.ds(pl.multiple_of(head_cols + g * N_STATE, N_STATE), N_STATE)]
        c_part = xc[:, pl.ds(pl.multiple_of(head_cols + (groups + g) * N_STATE, N_STATE), N_STATE)]
        products = dot_nt(c_part, b_part)
        cum_g = cum_row[group_rows(g), :]
        dt_g = dt_row[group_rows(g), :]
        skip_g = skip_row[group_rows(g), :]
        cum_t = jnp.transpose(cum_g)
        t_pos = lax.broadcasted_iota(jnp.int32, (rows, rows), 0)
        s_pos = lax.broadcasted_iota(jnp.int32, (rows, rows), 1)
        causal = s_pos <= t_pos
        low_half = lax.broadcasted_iota(jnp.int32, (rows, 2 * P_DIM), 1) < P_DIM
        for pair in range(per_group // 2):
            mixes = []
            for j in (2 * pair, 2 * pair + 1):
                gap = cum_t[:, j : j + 1] - cum_g[j : j + 1, :]
                decay = jnp.exp(jnp.where(causal, gap, NEG))
                mixes.append((products * decay * dt_g[j : j + 1, :]).astype(BF16))
            cols = pl.ds(pl.multiple_of(g * gcols + pair * 2 * P_DIM, 2 * P_DIM), 2 * P_DIM)
            x_pair = xc[:, cols].astype(F32)
            x_two = jnp.concatenate(
                [jnp.where(low_half, x_pair, 0.0), jnp.where(low_half, 0.0, x_pair)], axis=0
            ).astype(BF16)
            scale = jnp.where(
                low_half[:1], skip_g[2 * pair : 2 * pair + 1], skip_g[2 * pair + 1 : 2 * pair + 2]
            )
            y_acc[:, cols] = dot(jnp.concatenate(mixes, axis=1), x_two) + scale * x_pair

    pieces = kv_heads * 2
    piece_heads = repeat // 2
    log2_scale = 1.4426950408889634 / math.sqrt(KEY_DIM)

    def attn_flush(piece):
        width = piece_heads * KEY_DIM
        cols = pl.ds(pl.multiple_of(piece * width, width), width)
        return pltpu.make_async_copy(
            attn_out.at[:, cols], attn_hbm.at[:, cols], attn_sems.at[piece]
        )

    def attend(piece):
        kv_cols = pl.ds(pl.multiple_of((piece // 2) * KEY_DIM, KEY_DIM), KEY_DIM)
        k_all = jnp.concatenate([kbuf[j, :, kv_cols] for j in range(n)], axis=0)
        v_all = jnp.concatenate([vbuf[j, :, kv_cols] for j in range(n)], axis=0)
        q_pos = me * rows + lax.broadcasted_iota(jnp.int32, (rows, n * rows), 0)
        k_pos = lax.broadcasted_iota(jnp.int32, (rows, n * rows), 1)
        allowed = k_pos <= q_pos
        for j in range(piece_heads):
            start = (piece * piece_heads + j) * KEY_DIM
            cols = pl.ds(pl.multiple_of(start, KEY_DIM), KEY_DIM)
            scores = jnp.where(allowed, dot_nt(queries[:, cols], k_all), NEG)
            top = jnp.max(scores, axis=1, keepdims=True)
            probs = jnp.exp2((scores - top) * log2_scale)
            total = jnp.sum(probs, axis=1, keepdims=True)
            attn_out[:, cols] = (dot(probs.astype(BF16), v_all) / total).astype(BF16)
        attn_flush(piece).start()

    def mamba_flush(g):
        cols = pl.ds(pl.multiple_of(g * gcols, gcols), gcols)
        return pltpu.make_async_copy(
            mamba_out.at[:, cols], mamba_hbm.at[:, cols], mamba_sems.at[g]
        )

    def finish(g):
        cols = pl.ds(pl.multiple_of(g * gcols, gcols), gcols)
        v = y_acc[:, cols] * silu(gate[:, cols].astype(F32))
        scale = lax.rsqrt(jnp.mean(v * v, axis=1, keepdims=True) + EPS)
        mamba_out[:, cols] = (v * scale * gain[:, cols]).astype(BF16)
        mamba_flush(g).start()

    def chain(c, carry):
        g = c // per_chunks
        cols = pl.ds(pl.multiple_of(c * CHUNK, CHUNK), CHUNK)
        c_cols = pl.ds(pl.multiple_of(head_cols + (groups + g) * N_STATE, N_STATE), N_STATE)
        n_cols = pl.ds(pl.multiple_of(g * N_STATE, N_STATE), N_STATE)

        relay(c)

        def passed():
            total = ecum_x[rows - 1 : rows, cols]
            return (total * h_in[c].astype(F32) + s_own[c]).astype(BF16)

        @pl.when(has_prev & has_next)
        def _():
            h_copy(c).wait_recv()

        @pl.when(has_prev & (me < n - 2))
        def _():
            h_out[c] = passed()
            h_copy(c).start()

        @pl.when(before_last)
        def _():
            @pl.when(c == 0)
            def _():
                c_copy().wait_recv()

            r_out[c] = dot(c_next[:, n_cols], passed()).astype(BF16)
            r_copy(c).start()

        @pl.when((lax.rem(c, stride) == 0) & (c < stride * groups))
        def _():
            within(c // stride)

        @pl.when(has_prev & has_next)
        def _():
            y_acc[:, cols] += ecum_x[:, cols] * dot(xc[:, c_cols], h_in[c])

        @pl.when(is_last)
        def _():
            r_copy(c).wait_recv()
            y_acc[:, cols] += ecum_x[:, cols] * r_in[c].astype(F32)

        @pl.when(lax.rem(c, per_chunks) == per_chunks - 1)
        def _():
            finish(g)

        ahead = c - lead

        @pl.when((ahead >= 0) & (ahead < stride * pieces) & (lax.rem(ahead, stride) == 0))
        def _():
            attend(ahead // stride)

        return carry

    stride = 2
    lead = max(late + n - 1, stride * groups)
    lax.fori_loop(0, chunks, chain, 0)
    for c in range(chunks, late + n - 1):
        relay(c)

    def rest(piece, carry):
        attend(piece)
        return carry

    done = max(-(-(chunks - lead) // stride), 0)
    if done < pieces:
        lax.fori_loop(done, pieces, rest, 0)

    @pl.when(has_next)
    def _():
        rim_copy().wait_send()
        own_k().wait_send()
        own_v().wait_send()

        def sent_kv(block, carry):
            @pl.when(block < me)
            def _():
                k_copy(block).wait_send()
                v_copy(block).wait_send()

            return carry

        lax.fori_loop(0, n, sent_kv, 0)

    def sent_h(c, carry):
        h_copy(c).wait_send()
        return carry

    def sent_r(c, carry):
        r_copy(c).wait_send()
        return carry

    @pl.when(me < n - 2)
    def _():
        lax.fori_loop(0, chunks, sent_h, 0)

    @pl.when(before_last)
    def _():
        lax.fori_loop(0, chunks, sent_r, 0)

    @pl.when(is_last)
    def _():
        c_copy().wait_send()

    def out_done(g, carry):
        mamba_flush(g).wait()
        return carry

    def attn_done(piece, carry):
        attn_flush(piece).wait()
        return carry

    lax.fori_loop(0, pieces, attn_done, 0)
    lax.fori_loop(0, groups, out_done, 0)


def hand_on(mamba_src, attn_src, mamba_dst, attn_dst, mamba_mid, attn_mid, sems):
    quarter = mamba_src.shape[0] // 4
    loads, stores = [], []
    for i, (src, mid, dst) in enumerate(
        ((mamba_src, mamba_mid, mamba_dst), (attn_src, attn_mid, attn_dst))
    ):
        for j in range(4):
            part = pl.ds(j * quarter, quarter)
            k = 4 * i + j
            loads.append(
                pltpu.make_async_copy(src.at[part, :], mid.at[part, :], sems.at[0, k])
            )
            stores.append(
                pltpu.make_async_copy(mid.at[part, :], dst.at[part, :], sems.at[1, k])
            )
    for load in loads:
        load.start()
    for load, store in zip(loads, stores):
        load.wait()
        store.start()
    for store in stores:
        store.wait()


def shards(
    n,
    xbc,
    gate_in,
    dt_raw,
    dt_bias,
    a_log,
    conv_weight,
    conv_bias,
    skip_weight,
    norm_gain,
    queries,
    keys,
    values,
):
    rows = xbc.shape[0]
    heads = dt_raw.shape[0]
    head_cols = heads * P_DIM
    groups = (xbc.shape[1] - head_cols) // (2 * N_STATE)
    per_group = heads // groups
    chunks = head_cols // CHUNK
    hbm = pl.BlockSpec(memory_space=pltpu.HBM)
    dma = pltpu.SemaphoreType.DMA
    args = (
        xbc,
        gate_in,
        dt_raw,
        dt_bias.reshape(1, -1),
        a_log.reshape(1, -1),
        conv_weight,
        conv_bias.reshape(1, -1),
        skip_weight.reshape(1, -1),
        norm_gain.reshape(1, -1),
        queries,
        keys,
        values,
    )
    rim_rows = -(-(3 * (xbc.shape[1] // RIM_WIDTH)) // RIM) * RIM
    out_shape = (
        jax.ShapeDtypeStruct((rows, head_cols), BF16),
        jax.ShapeDtypeStruct(queries.shape, BF16),
    )
    outs = pl.pallas_call(
        functools.partial(kernel, n),
        out_shape=out_shape,
        in_specs=[hbm] * len(args),
        out_specs=(hbm, hbm),
        scratch_shapes=[
            pltpu.VMEM((rows, head_cols), BF16),
            pltpu.VMEM(queries.shape, BF16),
        ]
        + [pltpu.VMEM(a.shape, a.dtype) for a in args]
        + [
            pltpu.VMEM((RIM, xbc.shape[1]), BF16),
            pltpu.VMEM((8, xbc.shape[1]), F32),
            pltpu.VMEM((rim_rows, RIM_WIDTH), F32),
            pltpu.VMEM((rim_rows, RIM_WIDTH), BF16),
            pltpu.VMEM((rim_rows, RIM_WIDTH), BF16),
            pltpu.VMEM(xbc.shape, BF16),
            pltpu.VMEM((n,) + keys.shape, BF16),
            pltpu.VMEM((n,) + values.shape, BF16),
            pltpu.VMEM(dt_raw.shape, F32),
            pltpu.VMEM(dt_raw.shape, F32),
            pltpu.VMEM(dt_raw.shape, F32),
            pltpu.VMEM((rows, head_cols), F32),
            pltpu.VMEM((3 * per_group, per_group * P_DIM), BF16),
            pltpu.VMEM((chunks, N_STATE, CHUNK), F32),
            pltpu.VMEM((chunks, N_STATE, CHUNK), BF16),
            pltpu.VMEM((chunks, N_STATE, CHUNK), BF16),
            pltpu.VMEM((chunks, rows, CHUNK), BF16),
            pltpu.VMEM((chunks, rows, CHUNK), BF16),
            pltpu.VMEM((rows, groups * N_STATE), BF16),
            pltpu.VMEM((rows, head_cols), F32),
            dma((len(args) + 1,)),
            dma((groups,)),
            dma((2 * keys.shape[1] // KEY_DIM,)),
            dma,
            dma,
            dma((n,)),
            dma((n,)),
            dma((n,)),
            dma((n,)),
            dma((chunks,)),
            dma((chunks,)),
            dma((chunks,)),
            dma((chunks,)),
            dma,
            dma,
        ],
        compiler_params=pltpu.CompilerParams(
            collective_id=0, has_side_effects=True, vmem_limit_bytes=VMEM_BYTES
        ),
        name="mixers",
    )(*args)
    return pl.pallas_call(
        hand_on,
        out_shape=out_shape,
        in_specs=[hbm, hbm],
        out_specs=(hbm, hbm),
        scratch_shapes=[pltpu.VMEM(o.shape, BF16) for o in out_shape] + [dma((2, 8))],
        compiler_params=pltpu.CompilerParams(vmem_limit_bytes=VMEM_BYTES),
        name="hand_on",
    )(*outs)


def solution(mesh):
    placed = (
        P(("dp", "ctx"), "tp"),
        P(("dp", "ctx"), "tp"),
        P("tp", ("dp", "ctx")),
        P(("dp", "tp")),
        P("tp"),
        P(None, "tp"),
        P("tp"),
        P("tp"),
        P("tp"),
        P(("dp", "ctx"), "tp"),
        P(("dp", "ctx"), "tp"),
        P(("dp", "ctx"), "tp"),
    )
    return jax.shard_map(
        functools.partial(shards, mesh.shape["ctx"]),
        mesh=mesh,
        in_specs=placed,
        out_specs=(P(("dp", "ctx"), "tp"), P(("dp", "ctx"), "tp")),
        check_vma=False,
    )
```

```python
import functools
import math

import jax
import jax.numpy as jnp
from jax import lax
from jax.experimental import pallas as pl
from jax.experimental.pallas import tpu as pltpu
from jax.sharding import PartitionSpec as P

P_DIM = 64
N_STATE = 256
KEY_DIM = 128
CHUNK = 128
TILE = 256
RIM = 16
RIM_WIDTH = 384
VMEM_BYTES = 63 * 1024 * 1024
EPS = 1e-05
NEG = -1e30
F32 = jnp.float32
BF16 = jnp.bfloat16


def dot(a, b):
    return jnp.dot(a, b, preferred_element_type=F32)


def dot_nt(a, b):
    return lax.dot_general(a, b, (((1,), (1,)), ((), ())), preferred_element_type=F32)


def silu(v):
    return v / (1.0 + jnp.exp(-v))


def log1p_unit(e):
    z = e / (2.0 + e)
    z2 = z * z
    acc = jnp.full_like(z, 1.0 / 17.0)
    for k in (15, 13, 11, 9, 7, 5, 3, 1):
        acc = acc * z2 + 1.0 / k
    return 2.0 * z * acc


def kernel(
    n,
    xbc_hbm,
    gate_hbm,
    dt_hbm,
    bias_hbm,
    alog_hbm,
    convw_hbm,
    convb_hbm,
    skip_hbm,
    gain_hbm,
    queries_hbm,
    keys_hbm,
    values_hbm,
    mamba_hbm,
    attn_hbm,
    mamba_out,
    attn_out,
    xbc,
    gate,
    dt_raw,
    dt_bias,
    a_log,
    conv_w,
    conv_b,
    skip,
    gain,
    queries,
    keys,
    values,
    xbc_last,
    rim_wide,
    rim_tall,
    rim_src,
    rim_dst,
    xc,
    kbuf,
    vbuf,
    dt_row,
    cum_row,
    skip_row,
    ecum_x,
    spread,
    s_own,
    h_in,
    h_out,
    r_in,
    r_out,
    c_next,
    y_acc,
    in_sems,
    mamba_sems,
    attn_sems,
    rim_send,
    rim_recv,
    k_send,
    k_recv,
    v_send,
    v_recv,
    h_send,
    h_recv,
    r_send,
    r_recv,
    c_send,
    c_recv,
):
    me = lax.axis_index("ctx")
    rows = xbc.shape[0]
    heads = dt_raw.shape[0]
    head_cols = heads * P_DIM
    groups = (xbc.shape[1] - head_cols) // (2 * N_STATE)
    per_group = heads // groups
    gcols = per_group * P_DIM
    per_chunks = gcols // CHUNK
    chunks = groups * per_chunks
    taps = conv_w.shape[0]
    kv_heads = keys.shape[1] // KEY_DIM
    repeat = queries.shape[1] // keys.shape[1]
    has_next = me < n - 1
    has_prev = me > 0
    right = me + 1
    is_last = me == n - 1
    before_last = me == n - 2
    pieces_wide = xbc.shape[1] // RIM_WIDTH

    pairs = (
        (xbc_hbm.at[pl.ds(rows - RIM, RIM), :], xbc_last),
        (xbc_hbm, xbc),
        (dt_hbm, dt_raw),
        (bias_hbm, dt_bias),
        (alog_hbm, a_log),
        (convw_hbm, conv_w),
        (convb_hbm, conv_b),
        (skip_hbm, skip),
        (keys_hbm, keys),
        (values_hbm, values),
        (queries_hbm, queries),
        (gate_hbm, gate),
        (gain_hbm, gain),
    )
    loads = [pltpu.make_async_copy(a, b, in_sems.at[i]) for i, (a, b) in enumerate(pairs)]
    for load in loads:
        load.start()

    def remote(src, dst, send, recv, to):
        return pltpu.make_async_remote_copy(
            src_ref=src,
            dst_ref=dst,
            send_sem=send,
            recv_sem=recv,
            device_id={"ctx": to},
            device_id_type=pl.DeviceIdType.MESH,
        )

    barrier = pltpu.get_barrier_semaphore()

    @pl.when(has_prev)
    def _():
        pl.semaphore_signal(
            barrier, inc=1, device_id={"ctx": me - 1}, device_id_type=pl.DeviceIdType.MESH
        )

    @pl.when(before_last)
    def _():
        pl.semaphore_signal(
            barrier, inc=1, device_id={"ctx": me + 1}, device_id_type=pl.DeviceIdType.MESH
        )

    def rim_copy():
        return remote(rim_src, rim_dst, rim_send, rim_recv, right)

    def own_k():
        return remote(keys_hbm, kbuf.at[me], k_send.at[me], k_recv.at[me], right)

    def own_v():
        return remote(values_hbm, vbuf.at[me], v_send.at[me], v_recv.at[me], right)

    def k_copy(block):
        return remote(kbuf.at[block], kbuf.at[block], k_send.at[block], k_recv.at[block], right)

    def v_copy(block):
        return remote(vbuf.at[block], vbuf.at[block], v_send.at[block], v_recv.at[block], right)

    def h_copy(c):
        return remote(h_out.at[c], h_in.at[c], h_send.at[c], h_recv.at[c], right)

    def r_copy(c):
        return remote(r_out.at[c], r_in.at[c], r_send.at[c], r_recv.at[c], right)

    def c_copy():
        return remote(
            xc.at[:, pl.ds(head_cols + groups * N_STATE, groups * N_STATE)],
            c_next,
            c_send,
            c_recv,
            me - 1,
        )

    pl.semaphore_wait(barrier, 1)
    loads[0].wait()

    @pl.when(has_next)
    def _():
        last = xbc_last[...].astype(F32)
        for p in range(pieces_wide):
            rim_tall[p * 3 : p * 3 + 3, :] = last[
                RIM - 3 :, p * RIM_WIDTH : (p + 1) * RIM_WIDTH
            ]
        rim_src[...] = rim_tall[...].astype(BF16)
        rim_copy().start()
        own_k().start()

        @pl.when(has_prev)
        def _():
            own_v().start()

    def clear(j, carry):
        @pl.when(j > me)
        def _():
            kbuf[j] = jnp.zeros(keys.shape, BF16)
            vbuf[j] = jnp.zeros(values.shape, BF16)

        return carry

    lax.fori_loop(0, n, clear, 0)
    for load in loads[1:8]:
        load.wait()

    def column(ref):
        return jnp.transpose(jnp.broadcast_to(ref[...], (rows, heads)))

    pre = dt_raw[...] + column(dt_bias)
    dt = jnp.maximum(pre, 0.0) + log1p_unit(jnp.exp(-jnp.abs(pre)))
    cum = -dt * jnp.exp(column(a_log))
    lane = lax.broadcasted_iota(jnp.int32, (heads, rows), 1)
    step = 1
    while step < rows:
        cum = cum + jnp.where(lane >= step, pltpu.roll(cum, step, 1), 0.0)
        step *= 2
    skip_row[...] = column(skip)
    dt_row[...] = dt
    cum_row[...] = cum
    spread_row = lax.broadcasted_iota(jnp.int32, (3 * per_group, gcols), 0)
    spread_col = lax.broadcasted_iota(jnp.int32, (3 * per_group, gcols), 1)
    hit = lax.rem(spread_row, per_group) == spread_col // P_DIM
    spread[...] = jnp.where(hit, 1.0, 0.0).astype(BF16)

    def expand(v):
        hi = v.astype(BF16).astype(F32)
        rest = v - hi
        mid = rest.astype(BF16).astype(F32)
        low = rest - mid
        parts = jnp.transpose(jnp.concatenate([hi, mid, low], axis=0))
        return dot(parts.astype(BF16), spread[...])

    rim_wide[...] = jnp.zeros(rim_wide.shape, F32)

    @pl.when(has_prev)
    def _():
        rim_copy().wait_recv()
        rim_tall[...] = rim_dst[...].astype(F32)
        for p in range(pieces_wide):
            rim_wide[5:, p * RIM_WIDTH : (p + 1) * RIM_WIDTH] = rim_tall[p * 3 : p * 3 + 3, :]

    def conv_tile(start, width):
        cols = pl.ds(pl.multiple_of(start, 256), width)
        ext = jnp.concatenate([rim_wide[:, cols], xbc[:, cols].astype(F32)], axis=0)
        acc = jnp.broadcast_to(conv_b[:, cols], (rows, width))
        for tap in range(taps):
            by = taps - 1 - tap
            moved = ext if by == 0 else pltpu.roll(ext, by, 0)
            acc = acc + conv_w[tap : tap + 1, cols] * moved[8:]
        out = silu(acc)
        xc[:, cols] = out.astype(BF16)
        return out

    def passing(copy, block):
        @pl.when((block >= 0) & (block < me))
        def _():
            copy(block).wait_recv()

            @pl.when(has_next)
            def _():
                copy(block).start()

    late = per_chunks

    def relay(c):
        block = me - 1 - c

        @pl.when(c >= 1)
        def _():
            passing(k_copy, block)

            @pl.when(block >= 1)
            def _():
                passing(v_copy, block)

        @pl.when((me >= 1) & (c == late + me - 1))
        def _():
            passing(v_copy, 0)

    def group_rows(g):
        return pl.ds(pl.multiple_of(g * per_group, per_group), per_group)

    def first(g, carry):
        b_part = conv_tile(head_cols + g * N_STATE, N_STATE)
        b_turned = jnp.transpose(b_part).astype(BF16)
        cum_g = cum_row[group_rows(g), :]
        dt_g = dt_row[group_rows(g), :]
        last = jnp.broadcast_to(cum_g[:, rows - 1 :], cum_g.shape)
        tail = expand(dt_g * jnp.exp(last - cum_g))
        for i in range(gcols // TILE):
            x_part = conv_tile(g * gcols + i * TILE, TILE).astype(BF16).astype(F32)
            weighted = (x_part * tail[:, i * TILE : (i + 1) * TILE]).astype(BF16)
            own = dot(b_turned, weighted)
            for j in range(TILE // CHUNK):
                c = g * per_chunks + i * (TILE // CHUNK) + j
                s_own[c] = own[:, j * CHUNK : (j + 1) * CHUNK]

            @pl.when(me == 0)
            def _():
                for j in range(TILE // CHUNK):
                    c = g * per_chunks + i * (TILE // CHUNK) + j
                    h_out[c] = own[:, j * CHUNK : (j + 1) * CHUNK].astype(BF16)
                    h_copy(c).start()

        group_cols = pl.ds(pl.multiple_of(g * gcols, gcols), gcols)
        ecum_x[:, group_cols] = expand(jnp.exp(cum_g))
        y_acc[:, group_cols] = jnp.zeros((rows, gcols), F32)
        conv_tile(head_cols + (groups + g) * N_STATE, N_STATE)

        @pl.when((me == 0) & (g == 0))
        def _():
            own_v().start()

        @pl.when(g == min(1, groups - 1))
        def _():
            passing(k_copy, me - 1)

        @pl.when((g == groups - 1) & (me >= 2))
        def _():
            passing(v_copy, me - 1)

        return carry

    lax.fori_loop(0, groups, first, 0)

    @pl.when(is_last)
    def _():
        c_copy().start()

    for load in loads[8:]:
        load.wait()
    kbuf[me] = keys[...]
    vbuf[me] = values[...]

    def within(g):
        b_part = xc[:, pl.ds(pl.multiple_of(head_cols + g * N_STATE, N_STATE), N_STATE)]
        c_part = xc[:, pl.ds(pl.multiple_of(head_cols + (groups + g) * N_STATE, N_STATE), N_STATE)]
        products = dot_nt(c_part, b_part)
        cum_g = cum_row[group_rows(g), :]
        dt_g = dt_row[group_rows(g), :]
        skip_g = skip_row[group_rows(g), :]
        cum_t = jnp.transpose(cum_g)
        t_pos = lax.broadcasted_iota(jnp.int32, (rows, rows), 0)
        s_pos = lax.broadcasted_iota(jnp.int32, (rows, rows), 1)
        causal = s_pos <= t_pos
        low_half = lax.broadcasted_iota(jnp.int32, (rows, 2 * P_DIM), 1) < P_DIM
        for pair in range(per_group // 2):
            mixes = []
            for j in (2 * pair, 2 * pair + 1):
                gap = cum_t[:, j : j + 1] - cum_g[j : j + 1, :]
                decay = jnp.exp(jnp.where(causal, gap, NEG))
                mixes.append((products * decay * dt_g[j : j + 1, :]).astype(BF16))
            cols = pl.ds(pl.multiple_of(g * gcols + pair * 2 * P_DIM, 2 * P_DIM), 2 * P_DIM)
            x_pair = xc[:, cols].astype(F32)
            x_two = jnp.concatenate(
                [jnp.where(low_half, x_pair, 0.0), jnp.where(low_half, 0.0, x_pair)], axis=0
            ).astype(BF16)
            scale = jnp.where(
                low_half[:1], skip_g[2 * pair : 2 * pair + 1], skip_g[2 * pair + 1 : 2 * pair + 2]
            )
            y_acc[:, cols] += dot(jnp.concatenate(mixes, axis=1), x_two) + scale * x_pair

    pieces = kv_heads * 2
    piece_heads = repeat // 2
    log2_scale = 1.4426950408889634 / math.sqrt(KEY_DIM)

    def attn_flush(piece):
        width = piece_heads * KEY_DIM
        cols = pl.ds(pl.multiple_of(piece * width, width), width)
        return pltpu.make_async_copy(
            attn_out.at[:, cols], attn_hbm.at[:, cols], attn_sems.at[piece]
        )

    def attend(piece):
        kv_cols = pl.ds(pl.multiple_of((piece // 2) * KEY_DIM, KEY_DIM), KEY_DIM)
        k_all = jnp.concatenate([kbuf[j, :, kv_cols] for j in range(n)], axis=0)
        v_all = jnp.concatenate([vbuf[j, :, kv_cols] for j in range(n)], axis=0)
        q_pos = me * rows + lax.broadcasted_iota(jnp.int32, (rows, n * rows), 0)
        k_pos = lax.broadcasted_iota(jnp.int32, (rows, n * rows), 1)
        allowed = k_pos <= q_pos
        for j in range(piece_heads):
            start = (piece * piece_heads + j) * KEY_DIM
            cols = pl.ds(pl.multiple_of(start, KEY_DIM), KEY_DIM)
            scores = jnp.where(allowed, dot_nt(queries[:, cols], k_all), NEG)
            top = jnp.max(scores, axis=1, keepdims=True)
            probs = jnp.exp2((scores - top) * log2_scale)
            total = jnp.sum(probs, axis=1, keepdims=True)
            attn_out[:, cols] = (dot(probs.astype(BF16), v_all) / total).astype(BF16)
        attn_flush(piece).start()

    def mamba_flush(g):
        cols = pl.ds(pl.multiple_of(g * gcols, gcols), gcols)
        return pltpu.make_async_copy(
            mamba_out.at[:, cols], mamba_hbm.at[:, cols], mamba_sems.at[g]
        )

    def finish(g):
        cols = pl.ds(pl.multiple_of(g * gcols, gcols), gcols)
        v = y_acc[:, cols] * silu(gate[:, cols].astype(F32))
        scale = lax.rsqrt(jnp.mean(v * v, axis=1, keepdims=True) + EPS)
        mamba_out[:, cols] = (v * scale * gain[:, cols]).astype(BF16)
        mamba_flush(g).start()

    def chain(c, carry):
        g = c // per_chunks
        cols = pl.ds(pl.multiple_of(c * CHUNK, CHUNK), CHUNK)
        c_cols = pl.ds(pl.multiple_of(head_cols + (groups + g) * N_STATE, N_STATE), N_STATE)
        n_cols = pl.ds(pl.multiple_of(g * N_STATE, N_STATE), N_STATE)

        relay(c)

        def passed():
            total = ecum_x[rows - 1 : rows, cols]
            return (total * h_in[c].astype(F32) + s_own[c]).astype(BF16)

        @pl.when(has_prev & has_next)
        def _():
            h_copy(c).wait_recv()

        @pl.when(has_prev & (me < n - 2))
        def _():
            h_out[c] = passed()
            h_copy(c).start()

        @pl.when(before_last)
        def _():
            @pl.when(c == 0)
            def _():
                c_copy().wait_recv()

            r_out[c] = dot(c_next[:, n_cols], passed()).astype(BF16)
            r_copy(c).start()

        inner = c - wait_chunks

        @pl.when((inner >= 0) & (inner < stride * groups) & (lax.rem(inner, stride) == 0))
        def _():
            within(inner // stride)

        @pl.when(has_prev & has_next)
        def _():
            y_acc[:, cols] += ecum_x[:, cols] * dot(xc[:, c_cols], h_in[c])

        @pl.when(is_last)
        def _():
            r_copy(c).wait_recv()
            y_acc[:, cols] += ecum_x[:, cols] * r_in[c].astype(F32)

        @pl.when(lax.rem(c, per_chunks) == per_chunks - 1)
        def _():
            finish(g)

        ahead = c - lead

        @pl.when((ahead >= 0) & (ahead < stride * pieces) & (lax.rem(ahead, stride) == 0))
        def _():
            attend(ahead // stride)

        return carry

    stride = 2
    wait_chunks = min(4, per_chunks - 1)
    lead = max(late + n - 1, wait_chunks + stride * groups)
    lax.fori_loop(0, chunks, chain, 0)
    for c in range(chunks, late + n - 1):
        relay(c)

    def rest(piece, carry):
        attend(piece)
        return carry

    done = max(-(-(chunks - lead) // stride), 0)
    if done < pieces:
        lax.fori_loop(done, pieces, rest, 0)

    @pl.when(has_next)
    def _():
        rim_copy().wait_send()
        own_k().wait_send()
        own_v().wait_send()

        def sent_kv(block, carry):
            @pl.when(block < me)
            def _():
                k_copy(block).wait_send()
                v_copy(block).wait_send()

            return carry

        lax.fori_loop(0, n, sent_kv, 0)

    def sent_h(c, carry):
        h_copy(c).wait_send()
        return carry

    def sent_r(c, carry):
        r_copy(c).wait_send()
        return carry

    @pl.when(me < n - 2)
    def _():
        lax.fori_loop(0, chunks, sent_h, 0)

    @pl.when(before_last)
    def _():
        lax.fori_loop(0, chunks, sent_r, 0)

    @pl.when(is_last)
    def _():
        c_copy().wait_send()

    def out_done(g, carry):
        mamba_flush(g).wait()
        return carry

    def attn_done(piece, carry):
        attn_flush(piece).wait()
        return carry

    lax.fori_loop(0, pieces, attn_done, 0)
    lax.fori_loop(0, groups, out_done, 0)


def hand_on(mamba_src, attn_src, mamba_dst, attn_dst, mamba_mid, attn_mid, sems):
    quarter = mamba_src.shape[0] // 4
    loads, stores = [], []
    for i, (src, mid, dst) in enumerate(
        ((mamba_src, mamba_mid, mamba_dst), (attn_src, attn_mid, attn_dst))
    ):
        for j in range(4):
            part = pl.ds(j * quarter, quarter)
            k = 4 * i + j
            loads.append(
                pltpu.make_async_copy(src.at[part, :], mid.at[part, :], sems.at[0, k])
            )
            stores.append(
                pltpu.make_async_copy(mid.at[part, :], dst.at[part, :], sems.at[1, k])
            )
    for load in loads:
        load.start()
    for load, store in zip(loads, stores):
        load.wait()
        store.start()
    for store in stores:
        store.wait()


def shards(
    n,
    xbc,
    gate_in,
    dt_raw,
    dt_bias,
    a_log,
    conv_weight,
    conv_bias,
    skip_weight,
    norm_gain,
    queries,
    keys,
    values,
):
    rows = xbc.shape[0]
    heads = dt_raw.shape[0]
    head_cols = heads * P_DIM
    groups = (xbc.shape[1] - head_cols) // (2 * N_STATE)
    per_group = heads // groups
    chunks = head_cols // CHUNK
    hbm = pl.BlockSpec(memory_space=pltpu.HBM)
    dma = pltpu.SemaphoreType.DMA
    args = (
        xbc,
        gate_in,
        dt_raw,
        dt_bias.reshape(1, -1),
        a_log.reshape(1, -1),
        conv_weight,
        conv_bias.reshape(1, -1),
        skip_weight.reshape(1, -1),
        norm_gain.reshape(1, -1),
        queries,
        keys,
        values,
    )
    rim_rows = -(-(3 * (xbc.shape[1] // RIM_WIDTH)) // RIM) * RIM
    out_shape = (
        jax.ShapeDtypeStruct((rows, head_cols), BF16),
        jax.ShapeDtypeStruct(queries.shape, BF16),
    )
    outs = pl.pallas_call(
        functools.partial(kernel, n),
        out_shape=out_shape,
        in_specs=[hbm] * len(args),
        out_specs=(hbm, hbm),
        scratch_shapes=[
            pltpu.VMEM((rows, head_cols), BF16),
            pltpu.VMEM(queries.shape, BF16),
        ]
        + [pltpu.VMEM(a.shape, a.dtype) for a in args]
        + [
            pltpu.VMEM((RIM, xbc.shape[1]), BF16),
            pltpu.VMEM((8, xbc.shape[1]), F32),
            pltpu.VMEM((rim_rows, RIM_WIDTH), F32),
            pltpu.VMEM((rim_rows, RIM_WIDTH), BF16),
            pltpu.VMEM((rim_rows, RIM_WIDTH), BF16),
            pltpu.VMEM(xbc.shape, BF16),
            pltpu.VMEM((n,) + keys.shape, BF16),
            pltpu.VMEM((n,) + values.shape, BF16),
            pltpu.VMEM(dt_raw.shape, F32),
            pltpu.VMEM(dt_raw.shape, F32),
            pltpu.VMEM(dt_raw.shape, F32),
            pltpu.VMEM((rows, head_cols), F32),
            pltpu.VMEM((3 * per_group, per_group * P_DIM), BF16),
            pltpu.VMEM((chunks, N_STATE, CHUNK), F32),
            pltpu.VMEM((chunks, N_STATE, CHUNK), BF16),
            pltpu.VMEM((chunks, N_STATE, CHUNK), BF16),
            pltpu.VMEM((chunks, rows, CHUNK), BF16),
            pltpu.VMEM((chunks, rows, CHUNK), BF16),
            pltpu.VMEM((rows, groups * N_STATE), BF16),
            pltpu.VMEM((rows, head_cols), F32),
            dma((len(args) + 1,)),
            dma((groups,)),
            dma((2 * keys.shape[1] // KEY_DIM,)),
            dma,
            dma,
            dma((n,)),
            dma((n,)),
            dma((n,)),
            dma((n,)),
            dma((chunks,)),
            dma((chunks,)),
            dma((chunks,)),
            dma((chunks,)),
            dma,
            dma,
        ],
        compiler_params=pltpu.CompilerParams(
            collective_id=0, has_side_effects=True, vmem_limit_bytes=VMEM_BYTES
        ),
        name="mixers",
    )(*args)
    return pl.pallas_call(
        hand_on,
        out_shape=out_shape,
        in_specs=[hbm, hbm],
        out_specs=(hbm, hbm),
        scratch_shapes=[pltpu.VMEM(o.shape, BF16) for o in out_shape] + [dma((2, 8))],
        compiler_params=pltpu.CompilerParams(vmem_limit_bytes=VMEM_BYTES),
        name="hand_on",
    )(*outs)


def solution(mesh):
    placed = (
        P(("dp", "ctx"), "tp"),
        P(("dp", "ctx"), "tp"),
        P("tp", ("dp", "ctx")),
        P(("dp", "tp")),
        P("tp"),
        P(None, "tp"),
        P("tp"),
        P("tp"),
        P("tp"),
        P(("dp", "ctx"), "tp"),
        P(("dp", "ctx"), "tp"),
        P(("dp", "ctx"), "tp"),
    )
    return jax.shard_map(
        functools.partial(shards, mesh.shape["ctx"]),
        mesh=mesh,
        in_specs=placed,
        out_specs=(P(("dp", "ctx"), "tp"), P(("dp", "ctx"), "tp")),
        check_vma=False,
    )
```

```python
import functools
import math

import jax
import jax.numpy as jnp
from jax import lax
from jax.experimental import pallas as pl
from jax.experimental.pallas import tpu as pltpu
from jax.sharding import PartitionSpec as P

P_DIM = 64
N_STATE = 256
KEY_DIM = 128
CHUNK = 128
TILE = 256
RIM = 16
RIM_WIDTH = 384
VMEM_BYTES = 63 * 1024 * 1024
EPS = 1e-05
NEG = -1e30
F32 = jnp.float32
BF16 = jnp.bfloat16


def dot(a, b):
    return jnp.dot(a, b, preferred_element_type=F32)


def dot_nt(a, b):
    return lax.dot_general(a, b, (((1,), (1,)), ((), ())), preferred_element_type=F32)


def silu(v):
    return v / (1.0 + jnp.exp(-v))


def log1p_unit(e):
    z = e / (2.0 + e)
    z2 = z * z
    acc = jnp.full_like(z, 1.0 / 17.0)
    for k in (15, 13, 11, 9, 7, 5, 3, 1):
        acc = acc * z2 + 1.0 / k
    return 2.0 * z * acc


def kernel(
    n,
    xbc_hbm,
    gate_hbm,
    dt_hbm,
    bias_hbm,
    alog_hbm,
    convw_hbm,
    convb_hbm,
    skip_hbm,
    gain_hbm,
    queries_hbm,
    keys_hbm,
    values_hbm,
    mamba_hbm,
    attn_hbm,
    mamba_out,
    attn_out,
    xbc,
    gate,
    dt_raw,
    dt_bias,
    a_log,
    conv_w,
    conv_b,
    skip,
    gain,
    queries,
    keys,
    values,
    xbc_last,
    rim_wide,
    rim_tall,
    rim_src,
    rim_dst,
    xc,
    kbuf,
    vbuf,
    dt_row,
    cum_row,
    skip_row,
    ecum_x,
    spread,
    s_own,
    h_in,
    h_out,
    r_in,
    r_out,
    c_next,
    y_acc,
    in_sems,
    mamba_sems,
    attn_sems,
    rim_send,
    rim_recv,
    k_send,
    k_recv,
    v_send,
    v_recv,
    h_send,
    h_recv,
    r_send,
    r_recv,
    c_send,
    c_recv,
):
    me = lax.axis_index("ctx")
    rows = xbc.shape[0]
    heads = dt_raw.shape[0]
    head_cols = heads * P_DIM
    groups = (xbc.shape[1] - head_cols) // (2 * N_STATE)
    per_group = heads // groups
    gcols = per_group * P_DIM
    per_chunks = gcols // CHUNK
    chunks = groups * per_chunks
    taps = conv_w.shape[0]
    kv_heads = keys.shape[1] // KEY_DIM
    repeat = queries.shape[1] // keys.shape[1]
    has_next = me < n - 1
    has_prev = me > 0
    right = me + 1
    is_last = me == n - 1
    before_last = me == n - 2
    pieces_wide = xbc.shape[1] // RIM_WIDTH

    pairs = (
        (xbc_hbm.at[pl.ds(rows - RIM, RIM), :], xbc_last),
        (xbc_hbm, xbc),
        (dt_hbm, dt_raw),
        (bias_hbm, dt_bias),
        (alog_hbm, a_log),
        (convw_hbm, conv_w),
        (convb_hbm, conv_b),
        (skip_hbm, skip),
        (keys_hbm, keys),
        (values_hbm, values),
        (queries_hbm, queries),
        (gate_hbm, gate),
        (gain_hbm, gain),
    )
    loads = [pltpu.make_async_copy(a, b, in_sems.at[i]) for i, (a, b) in enumerate(pairs)]
    for load in loads:
        load.start()

    def remote(src, dst, send, recv, to):
        return pltpu.make_async_remote_copy(
            src_ref=src,
            dst_ref=dst,
            send_sem=send,
            recv_sem=recv,
            device_id={"ctx": to},
            device_id_type=pl.DeviceIdType.MESH,
        )

    barrier = pltpu.get_barrier_semaphore()

    @pl.when(has_prev)
    def _():
        pl.semaphore_signal(
            barrier, inc=1, device_id={"ctx": me - 1}, device_id_type=pl.DeviceIdType.MESH
        )

    @pl.when(before_last)
    def _():
        pl.semaphore_signal(
            barrier, inc=1, device_id={"ctx": me + 1}, device_id_type=pl.DeviceIdType.MESH
        )

    def rim_copy():
        return remote(rim_src, rim_dst, rim_send, rim_recv, right)

    def own_k():
        return remote(keys_hbm, kbuf.at[me], k_send.at[me], k_recv.at[me], right)

    def own_v():
        return remote(values_hbm, vbuf.at[me], v_send.at[me], v_recv.at[me], right)

    def k_copy(block):
        return remote(kbuf.at[block], kbuf.at[block], k_send.at[block], k_recv.at[block], right)

    def v_copy(block):
        return remote(vbuf.at[block], vbuf.at[block], v_send.at[block], v_recv.at[block], right)

    def h_copy(c):
        return remote(h_out.at[c], h_in.at[c], h_send.at[c], h_recv.at[c], right)

    def r_copy(c):
        return remote(r_out.at[c], r_in.at[c], r_send.at[c], r_recv.at[c], right)

    def c_copy():
        return remote(
            xc.at[:, pl.ds(head_cols + groups * N_STATE, groups * N_STATE)],
            c_next,
            c_send,
            c_recv,
            me - 1,
        )

    pl.semaphore_wait(barrier, 1)

    @pl.when(has_next)
    def _():
        @pl.when(has_prev)
        def _():
            own_k().start()

        loads[0].wait()
        last = xbc_last[...].astype(F32)
        for p in range(pieces_wide):
            rim_tall[p * 3 : p * 3 + 3, :] = last[
                RIM - 3 :, p * RIM_WIDTH : (p + 1) * RIM_WIDTH
            ]
        rim_src[...] = rim_tall[...].astype(BF16)
        rim_copy().start()

        @pl.when(me == 0)
        def _():
            own_k().start()

        @pl.when(has_prev)
        def _():
            own_v().start()

    @pl.when(is_last)
    def _():
        loads[0].wait()

    def clear(j, carry):
        @pl.when(j > me)
        def _():
            kbuf[j] = jnp.zeros(keys.shape, BF16)
            vbuf[j] = jnp.zeros(values.shape, BF16)

        return carry

    lax.fori_loop(0, n, clear, 0)
    for load in loads[1:8]:
        load.wait()

    def column(ref):
        return jnp.transpose(jnp.broadcast_to(ref[...], (rows, heads)))

    pre = dt_raw[...] + column(dt_bias)
    dt = jnp.maximum(pre, 0.0) + log1p_unit(jnp.exp(-jnp.abs(pre)))
    cum = -dt * jnp.exp(column(a_log))
    lane = lax.broadcasted_iota(jnp.int32, (heads, rows), 1)
    step = 1
    while step < rows:
        cum = cum + jnp.where(lane >= step, pltpu.roll(cum, step, 1), 0.0)
        step *= 2
    skip_row[...] = column(skip)
    dt_row[...] = dt
    cum_row[...] = cum
    spread_row = lax.broadcasted_iota(jnp.int32, (3 * per_group, gcols), 0)
    spread_col = lax.broadcasted_iota(jnp.int32, (3 * per_group, gcols), 1)
    hit = lax.rem(spread_row, per_group) == spread_col // P_DIM
    spread[...] = jnp.where(hit, 1.0, 0.0).astype(BF16)

    def expand(v):
        hi = v.astype(BF16).astype(F32)
        rest = v - hi
        mid = rest.astype(BF16).astype(F32)
        low = rest - mid
        parts = jnp.transpose(jnp.concatenate([hi, mid, low], axis=0))
        return dot(parts.astype(BF16), spread[...])

    rim_wide[...] = jnp.zeros(rim_wide.shape, F32)

    @pl.when(has_prev)
    def _():
        rim_copy().wait_recv()
        rim_tall[...] = rim_dst[...].astype(F32)
        for p in range(pieces_wide):
            rim_wide[5:, p * RIM_WIDTH : (p + 1) * RIM_WIDTH] = rim_tall[p * 3 : p * 3 + 3, :]

    def conv_tile(start, width):
        cols = pl.ds(pl.multiple_of(start, 256), width)
        ext = jnp.concatenate([rim_wide[:, cols], xbc[:, cols].astype(F32)], axis=0)
        acc = jnp.broadcast_to(conv_b[:, cols], (rows, width))
        for tap in range(taps):
            by = taps - 1 - tap
            moved = ext if by == 0 else pltpu.roll(ext, by, 0)
            acc = acc + conv_w[tap : tap + 1, cols] * moved[8:]
        out = silu(acc)
        xc[:, cols] = out.astype(BF16)
        return out

    def passing(copy, block):
        @pl.when((block >= 0) & (block < me))
        def _():
            copy(block).wait_recv()

            @pl.when(has_next)
            def _():
                copy(block).start()

    late = per_chunks

    def relay(c):
        block = me - 1 - c

        @pl.when(c >= 1)
        def _():
            passing(k_copy, block)

            @pl.when(block >= 1)
            def _():
                passing(v_copy, block)

        @pl.when((me >= 1) & (c == late + me - 1))
        def _():
            passing(v_copy, 0)

    def group_rows(g):
        return pl.ds(pl.multiple_of(g * per_group, per_group), per_group)

    def first(g, carry):
        b_part = conv_tile(head_cols + g * N_STATE, N_STATE)
        b_turned = jnp.transpose(b_part).astype(BF16)
        cum_g = cum_row[group_rows(g), :]
        dt_g = dt_row[group_rows(g), :]
        last = jnp.broadcast_to(cum_g[:, rows - 1 :], cum_g.shape)
        tail = expand(dt_g * jnp.exp(last - cum_g))
        for i in range(gcols // TILE):
            x_part = conv_tile(g * gcols + i * TILE, TILE).astype(BF16).astype(F32)
            weighted = (x_part * tail[:, i * TILE : (i + 1) * TILE]).astype(BF16)
            own = dot(b_turned, weighted)
            for j in range(TILE // CHUNK):
                c = g * per_chunks + i * (TILE // CHUNK) + j
                s_own[c] = own[:, j * CHUNK : (j + 1) * CHUNK]

            @pl.when(me == 0)
            def _():
                for j in range(TILE // CHUNK):
                    c = g * per_chunks + i * (TILE // CHUNK) + j
                    h_out[c] = own[:, j * CHUNK : (j + 1) * CHUNK].astype(BF16)
                    h_copy(c).start()

        group_cols = pl.ds(pl.multiple_of(g * gcols, gcols), gcols)
        ecum_x[:, group_cols] = expand(jnp.exp(cum_g))
        y_acc[:, group_cols] = jnp.zeros((rows, gcols), F32)
        conv_tile(head_cols + (groups + g) * N_STATE, N_STATE)

        @pl.when((me == 0) & (g == 0))
        def _():
            own_v().start()

        @pl.when(g == min(1, groups - 1))
        def _():
            passing(k_copy, me - 1)

        @pl.when((g == groups - 1) & (me >= 2))
        def _():
            passing(v_copy, me - 1)

        return carry

    lax.fori_loop(0, groups, first, 0)

    @pl.when(is_last)
    def _():
        c_copy().start()

    for load in loads[8:]:
        load.wait()
    kbuf[me] = keys[...]
    vbuf[me] = values[...]

    def within(g):
        b_part = xc[:, pl.ds(pl.multiple_of(head_cols + g * N_STATE, N_STATE), N_STATE)]
        c_part = xc[:, pl.ds(pl.multiple_of(head_cols + (groups + g) * N_STATE, N_STATE), N_STATE)]
        products = dot_nt(c_part, b_part)
        cum_g = cum_row[group_rows(g), :]
        dt_g = dt_row[group_rows(g), :]
        skip_g = skip_row[group_rows(g), :]
        cum_t = jnp.transpose(cum_g)
        t_pos = lax.broadcasted_iota(jnp.int32, (rows, rows), 0)
        s_pos = lax.broadcasted_iota(jnp.int32, (rows, rows), 1)
        causal = s_pos <= t_pos
        low_half = lax.broadcasted_iota(jnp.int32, (rows, 2 * P_DIM), 1) < P_DIM
        for pair in range(per_group // 2):
            mixes = []
            for j in (2 * pair, 2 * pair + 1):
                gap = cum_t[:, j : j + 1] - cum_g[j : j + 1, :]
                decay = jnp.exp(jnp.where(causal, gap, NEG))
                mixes.append((products * decay * dt_g[j : j + 1, :]).astype(BF16))
            cols = pl.ds(pl.multiple_of(g * gcols + pair * 2 * P_DIM, 2 * P_DIM), 2 * P_DIM)
            x_pair = xc[:, cols].astype(F32)
            x_two = jnp.concatenate(
                [jnp.where(low_half, x_pair, 0.0), jnp.where(low_half, 0.0, x_pair)], axis=0
            ).astype(BF16)
            scale = jnp.where(
                low_half[:1], skip_g[2 * pair : 2 * pair + 1], skip_g[2 * pair + 1 : 2 * pair + 2]
            )
            y_acc[:, cols] += dot(jnp.concatenate(mixes, axis=1), x_two) + scale * x_pair

    pieces = kv_heads * 2
    piece_heads = repeat // 2
    log2_scale = 1.4426950408889634 / math.sqrt(KEY_DIM)

    def attn_flush(piece):
        width = piece_heads * KEY_DIM
        cols = pl.ds(pl.multiple_of(piece * width, width), width)
        return pltpu.make_async_copy(
            attn_out.at[:, cols], attn_hbm.at[:, cols], attn_sems.at[piece]
        )

    def attend(piece):
        kv_cols = pl.ds(pl.multiple_of((piece // 2) * KEY_DIM, KEY_DIM), KEY_DIM)
        k_all = jnp.concatenate([kbuf[j, :, kv_cols] for j in range(n)], axis=0)
        v_all = jnp.concatenate([vbuf[j, :, kv_cols] for j in range(n)], axis=0)
        q_pos = me * rows + lax.broadcasted_iota(jnp.int32, (rows, n * rows), 0)
        k_pos = lax.broadcasted_iota(jnp.int32, (rows, n * rows), 1)
        allowed = k_pos <= q_pos
        for j in range(piece_heads):
            start = (piece * piece_heads + j) * KEY_DIM
            cols = pl.ds(pl.multiple_of(start, KEY_DIM), KEY_DIM)
            scores = jnp.where(allowed, dot_nt(queries[:, cols], k_all), NEG)
            top = jnp.max(scores, axis=1, keepdims=True)
            probs = jnp.exp2((scores - top) * log2_scale)
            total = jnp.sum(probs, axis=1, keepdims=True)
            attn_out[:, cols] = (dot(probs.astype(BF16), v_all) / total).astype(BF16)
        attn_flush(piece).start()

    def mamba_flush(g):
        cols = pl.ds(pl.multiple_of(g * gcols, gcols), gcols)
        return pltpu.make_async_copy(
            mamba_out.at[:, cols], mamba_hbm.at[:, cols], mamba_sems.at[g]
        )

    def finish(g):
        cols = pl.ds(pl.multiple_of(g * gcols, gcols), gcols)
        v = y_acc[:, cols] * silu(gate[:, cols].astype(F32))
        scale = lax.rsqrt(jnp.mean(v * v, axis=1, keepdims=True) + EPS)
        mamba_out[:, cols] = (v * scale * gain[:, cols]).astype(BF16)
        mamba_flush(g).start()

    def chain(c, carry):
        g = c // per_chunks
        cols = pl.ds(pl.multiple_of(c * CHUNK, CHUNK), CHUNK)
        c_cols = pl.ds(pl.multiple_of(head_cols + (groups + g) * N_STATE, N_STATE), N_STATE)
        n_cols = pl.ds(pl.multiple_of(g * N_STATE, N_STATE), N_STATE)

        relay(c)

        def passed():
            total = ecum_x[rows - 1 : rows, cols]
            return (total * h_in[c].astype(F32) + s_own[c]).astype(BF16)

        @pl.when(has_prev & has_next)
        def _():
            h_copy(c).wait_recv()

        @pl.when(has_prev & (me < n - 2))
        def _():
            h_out[c] = passed()
            h_copy(c).start()

        @pl.when(before_last)
        def _():
            @pl.when(c == 0)
            def _():
                c_copy().wait_recv()

            r_out[c] = dot(c_next[:, n_cols], passed()).astype(BF16)
            r_copy(c).start()

        inner = c - wait_chunks

        @pl.when((inner >= 0) & (inner < stride * groups) & (lax.rem(inner, stride) == 0))
        def _():
            within(inner // stride)

        @pl.when(has_prev & has_next)
        def _():
            y_acc[:, cols] += ecum_x[:, cols] * dot(xc[:, c_cols], h_in[c])

        @pl.when(is_last)
        def _():
            r_copy(c).wait_recv()
            y_acc[:, cols] += ecum_x[:, cols] * r_in[c].astype(F32)

        @pl.when(lax.rem(c, per_chunks) == per_chunks - 1)
        def _():
            finish(g)

        ahead = c - lead

        @pl.when((ahead >= 0) & (ahead < stride * pieces) & (lax.rem(ahead, stride) == 0))
        def _():
            attend(ahead // stride)

        return carry

    stride = 2
    wait_chunks = min(4, per_chunks - 1)
    lead = max(late + n - 1, wait_chunks + stride * groups)
    lax.fori_loop(0, chunks, chain, 0)
    for c in range(chunks, late + n - 1):
        relay(c)

    def rest(piece, carry):
        attend(piece)
        return carry

    done = max(-(-(chunks - lead) // stride), 0)
    if done < pieces:
        lax.fori_loop(done, pieces, rest, 0)

    @pl.when(has_next)
    def _():
        rim_copy().wait_send()
        own_k().wait_send()
        own_v().wait_send()

        def sent_kv(block, carry):
            @pl.when(block < me)
            def _():
                k_copy(block).wait_send()
                v_copy(block).wait_send()

            return carry

        lax.fori_loop(0, n, sent_kv, 0)

    def sent_h(c, carry):
        h_copy(c).wait_send()
        return carry

    def sent_r(c, carry):
        r_copy(c).wait_send()
        return carry

    @pl.when(me < n - 2)
    def _():
        lax.fori_loop(0, chunks, sent_h, 0)

    @pl.when(before_last)
    def _():
        lax.fori_loop(0, chunks, sent_r, 0)

    @pl.when(is_last)
    def _():
        c_copy().wait_send()

    def out_done(g, carry):
        mamba_flush(g).wait()
        return carry

    def attn_done(piece, carry):
        attn_flush(piece).wait()
        return carry

    lax.fori_loop(0, pieces, attn_done, 0)
    lax.fori_loop(0, groups, out_done, 0)


def hand_on(mamba_src, attn_src, mamba_dst, attn_dst, mamba_mid, attn_mid, sems):
    quarter = mamba_src.shape[0] // 4
    loads, stores = [], []
    for i, (src, mid, dst) in enumerate(
        ((mamba_src, mamba_mid, mamba_dst), (attn_src, attn_mid, attn_dst))
    ):
        for j in range(4):
            part = pl.ds(j * quarter, quarter)
            k = 4 * i + j
            loads.append(
                pltpu.make_async_copy(src.at[part, :], mid.at[part, :], sems.at[0, k])
            )
            stores.append(
                pltpu.make_async_copy(mid.at[part, :], dst.at[part, :], sems.at[1, k])
            )
    for load in loads:
        load.start()
    for load, store in zip(loads, stores):
        load.wait()
        store.start()
    for store in stores:
        store.wait()


def shards(
    n,
    xbc,
    gate_in,
    dt_raw,
    dt_bias,
    a_log,
    conv_weight,
    conv_bias,
    skip_weight,
    norm_gain,
    queries,
    keys,
    values,
):
    rows = xbc.shape[0]
    heads = dt_raw.shape[0]
    head_cols = heads * P_DIM
    groups = (xbc.shape[1] - head_cols) // (2 * N_STATE)
    per_group = heads // groups
    chunks = head_cols // CHUNK
    hbm = pl.BlockSpec(memory_space=pltpu.HBM)
    dma = pltpu.SemaphoreType.DMA
    args = (
        xbc,
        gate_in,
        dt_raw,
        dt_bias.reshape(1, -1),
        a_log.reshape(1, -1),
        conv_weight,
        conv_bias.reshape(1, -1),
        skip_weight.reshape(1, -1),
        norm_gain.reshape(1, -1),
        queries,
        keys,
        values,
    )
    rim_rows = -(-(3 * (xbc.shape[1] // RIM_WIDTH)) // RIM) * RIM
    out_shape = (
        jax.ShapeDtypeStruct((rows, head_cols), BF16),
        jax.ShapeDtypeStruct(queries.shape, BF16),
    )
    outs = pl.pallas_call(
        functools.partial(kernel, n),
        out_shape=out_shape,
        in_specs=[hbm] * len(args),
        out_specs=(hbm, hbm),
        scratch_shapes=[
            pltpu.VMEM((rows, head_cols), BF16),
            pltpu.VMEM(queries.shape, BF16),
        ]
        + [pltpu.VMEM(a.shape, a.dtype) for a in args]
        + [
            pltpu.VMEM((RIM, xbc.shape[1]), BF16),
            pltpu.VMEM((8, xbc.shape[1]), F32),
            pltpu.VMEM((rim_rows, RIM_WIDTH), F32),
            pltpu.VMEM((rim_rows, RIM_WIDTH), BF16),
            pltpu.VMEM((rim_rows, RIM_WIDTH), BF16),
            pltpu.VMEM(xbc.shape, BF16),
            pltpu.VMEM((n,) + keys.shape, BF16),
            pltpu.VMEM((n,) + values.shape, BF16),
            pltpu.VMEM(dt_raw.shape, F32),
            pltpu.VMEM(dt_raw.shape, F32),
            pltpu.VMEM(dt_raw.shape, F32),
            pltpu.VMEM((rows, head_cols), F32),
            pltpu.VMEM((3 * per_group, per_group * P_DIM), BF16),
            pltpu.VMEM((chunks, N_STATE, CHUNK), F32),
            pltpu.VMEM((chunks, N_STATE, CHUNK), BF16),
            pltpu.VMEM((chunks, N_STATE, CHUNK), BF16),
            pltpu.VMEM((chunks, rows, CHUNK), BF16),
            pltpu.VMEM((chunks, rows, CHUNK), BF16),
            pltpu.VMEM((rows, groups * N_STATE), BF16),
            pltpu.VMEM((rows, head_cols), F32),
            dma((len(args) + 1,)),
            dma((groups,)),
            dma((2 * keys.shape[1] // KEY_DIM,)),
            dma,
            dma,
            dma((n,)),
            dma((n,)),
            dma((n,)),
            dma((n,)),
            dma((chunks,)),
            dma((chunks,)),
            dma((chunks,)),
            dma((chunks,)),
            dma,
            dma,
        ],
        compiler_params=pltpu.CompilerParams(
            collective_id=0, has_side_effects=True, vmem_limit_bytes=VMEM_BYTES
        ),
        name="mixers",
    )(*args)
    return pl.pallas_call(
        hand_on,
        out_shape=out_shape,
        in_specs=[hbm, hbm],
        out_specs=(hbm, hbm),
        scratch_shapes=[pltpu.VMEM(o.shape, BF16) for o in out_shape] + [dma((2, 8))],
        compiler_params=pltpu.CompilerParams(vmem_limit_bytes=VMEM_BYTES),
        name="hand_on",
    )(*outs)


def solution(mesh):
    placed = (
        P(("dp", "ctx"), "tp"),
        P(("dp", "ctx"), "tp"),
        P("tp", ("dp", "ctx")),
        P(("dp", "tp")),
        P("tp"),
        P(None, "tp"),
        P("tp"),
        P("tp"),
        P("tp"),
        P(("dp", "ctx"), "tp"),
        P(("dp", "ctx"), "tp"),
        P(("dp", "ctx"), "tp"),
    )
    return jax.shard_map(
        functools.partial(shards, mesh.shape["ctx"]),
        mesh=mesh,
        in_specs=placed,
        out_specs=(P(("dp", "ctx"), "tp"), P(("dp", "ctx"), "tp")),
        check_vma=False,
    )
```
